32 devices in a mesh: groups: 2 (over y), seq: 4 (over z), adapter: 2 (over x), head: 2 (over core).
Axes of the slice: x: 2, y: 2, z: 4, core: 2. Of those that a mesh axis runs over, the one named last changes fastest.
Arguments:
- hidden: bfloat16 [64, 3, 8192], P(('groups', 'seq', 'adapter'), None, 'head'), parts along dimension 0, may hold values from -6 to 6
- base_query_rows: bfloat16 [64, 3, 8192], P(('groups', 'seq', 'adapter'), None, 'head'), parts along dimension 0, may hold values from -16 to 16
- fresh_key_value: bfloat16 [2, 64, 3, 1024], P(None, ('groups', 'seq', 'adapter'), None, 'head'), parts along dimension 1, may hold values from -12 to 12
- suffix_key_value: bfloat16 [2, 64, 32, 1024], P(None, ('groups', 'seq', 'adapter'), None, 'head'), parts along dimension 1, may hold values from -12 to 12
- suffix_length: int32 [64], P(('groups', 'seq', 'adapter')), parts along dimension 0, may hold values from 0 to 32, as said below
- row_adapter_index: int32 [64, 1], P(('groups', 'seq', 'adapter')), parts along dimension 0, may hold values from 0 to 1
- prompt_key_value: bfloat16 [2, 8192, 1024], P(None, ('groups', 'seq'), 'head'), parts along dimension 1, may hold values from -16 to 16
- query_down_factors: bfloat16 [4, 64, 8192], P(('groups', 'adapter'), None, 'head'), parts along dimension 0, may hold values from -0.0625 to 0.0625
- query_up_factors: bfloat16 [4, 64, 8192], P(('groups', 'adapter'), None, 'head'), parts along dimension 0, may hold values from -0.75 to 0.75
- output_down_factors: bfloat16 [4, 64, 8192], P(('groups', 'adapter'), None, 'head'), parts along dimension 0, may hold values from -0.0625 to 0.0625
- output_up_factors: bfloat16 [4, 64, 8192], P(('groups', 'adapter'), None, 'head'), parts along dimension 0, may hold values from -0.75 to 0.75
Outputs:
- attended: bfloat16 [64, 3, 8192], P(('groups', 'seq', 'adapter'), None, 'head'), parts along dimension 0
- adapted: bfloat16 [64, 3, 8192], P(('groups', 'seq', 'adapter'), None, 'head'), parts along dimension 0
The draws below stay inside these ranges and needn't reach their ends.
There are 2 independent parts, one for each index of `groups`. The reference program is written for one: setup_inputs(seed, part) draws one part's arguments, and reference() takes and returns one part's arrays. A program takes and returns all parts, laid end to end along the dimension named above; each array names one. Nothing has to cross between parts.
Inputs may be any that keep to these rules, and one draw needn't show every extreme that they name: `suffix_length`: each row's suffix holds at most 32 tokens, and some row holds exactly 32.
All inputs are finite; a program needn't handle non-finite values.
Results may differ from the reference program's by a relative error of at most 0.011.
Values may be sent and summed in bfloat16 or wider, within the bound.
No kernel may reach another device: no remote copies, remote signals or barrier semaphores. Data moves between devices by JAX's collectives and lax.ppermute only.
A program may use at most 64 MiB of HBM per device.

```python
import math
import jax
import jax.numpy as jnp
from jax import lax

MODEL_WIDTH = 8192
QUERY_HEADS = 64
KVH = 8
HEAD_SIZE = 128
FACTOR_RANK = 64
STEPS = 3
P_DEV = 1024
SUF = 32
ADAPTER_TOTAL = 2
ROWS = 32
PROMPT = 4096
N_SEQ = 4


def draw_base_query_rows(key, part):
    values = jax.random.truncated_normal(key, -6.0, 6.0, (ROWS, STEPS, QUERY_HEADS, HEAD_SIZE), jnp.float32)
    return values.reshape(ROWS, STEPS, QUERY_HEADS * HEAD_SIZE).astype(jnp.bfloat16)


def draw_prompt_key_value(key, part):
    first_key, second_key = jax.random.split(jax.random.fold_in(key, 17))
    keys_part = 2.0 * jax.random.truncated_normal(first_key, -8.0, 8.0, (PROMPT, KVH, HEAD_SIZE), jnp.float32)
    values_part = jax.random.truncated_normal(second_key, -6.0, 6.0, (PROMPT, KVH * HEAD_SIZE), jnp.float32)
    return jnp.stack([keys_part.reshape(PROMPT, KVH * HEAD_SIZE), values_part]).astype(jnp.bfloat16)


def draw_suffix_length(key, part):
    lengths = jax.random.randint(jax.random.fold_in(key, 29), (ROWS,), 0, SUF + 1)
    return lengths.at[0].set(SUF)


def block_scale(rng, extent, cuts, smallest, high):
    factor_of = 1.0
    for axis_at, blocks in cuts:
        heights = jax.random.uniform(jax.random.fold_in(jax.random.fold_in(rng, 6), axis_at), (blocks,), jnp.float32, smallest / len(cuts), high / len(cuts))
        factor_of = factor_of * jnp.repeat(jnp.exp(heights), extent[axis_at] // blocks).reshape((-1,) + (1,) * (len(extent) - 1 - axis_at))
    return factor_of


def choose_distinct(stream_key, rows, amount, top, lift):
    sequence = jax.random.permutation(jax.random.fold_in(stream_key, 1), amount)
    favour = sequence
    for power in range(3):
        favour = favour * favour // amount
    favour = favour * lift // amount
    tickets = jax.random.randint(jax.random.fold_in(stream_key, 2), (rows, amount), 0, 4096) + favour
    fixed_rows = jax.random.permutation(jax.random.fold_in(stream_key, 3), rows)[jnp.arange(amount) % rows]
    tickets = jnp.where(jnp.arange(rows)[:, None] == fixed_rows[None, :], 1 << 14, tickets)
    priority = tickets * amount + jnp.arange(amount)
    return lax.top_k(priority.astype(jnp.int32), top)[1].astype(jnp.int32)


def gaussian(key, shape, width, most, cuts=(), kind=jnp.bfloat16):
    values = jax.random.normal(key, shape, jnp.float32) * width
    if len(cuts) > 0:
        values = block_scale(key, shape, cuts, -0.22, 0.18) * values
    return jnp.clip(values, min=-most, max=most).astype(kind)


def setup_inputs(seed: int = 0, part: int = 0) -> dict:
    streams_of = jax.random.split(jax.random.key(seed), 12)
    part_splits = jax.random.split(jax.random.fold_in(streams_of[11], part), 12)
    hidden = gaussian(part_splits[0], (ROWS, STEPS, MODEL_WIDTH), 1.0, 6.0, ((0, 8), (2, 2)))
    base_query_rows = draw_base_query_rows(jax.random.fold_in(jax.random.fold_in(streams_of[11], part), 71), part)
    fresh_key_value = gaussian(part_splits[2], (2, ROWS, STEPS, KVH * HEAD_SIZE), 2.0, 12.0, ((1, 8), (3, 2)))
    suffix_key_value = gaussian(part_splits[3], (2, ROWS, SUF, KVH * HEAD_SIZE), 2.0, 12.0, ((1, 8), (3, 2)))
    suffix_length = draw_suffix_length(jax.random.fold_in(jax.random.fold_in(streams_of[11], part), 71), part)
    row_adapter_index = choose_distinct(part_splits[5], ROWS, ADAPTER_TOTAL, 1, 4096)
    prompt_key_value = draw_prompt_key_value(jax.random.fold_in(jax.random.fold_in(streams_of[11], part), 71), part)
    query_down_factors = gaussian(part_splits[7], (ADAPTER_TOTAL, FACTOR_RANK, MODEL_WIDTH), MODEL_WIDTH ** -0.5, 0.0625, ((0, 2), (2, 2)))
    query_up_factors = gaussian(part_splits[8], (ADAPTER_TOTAL, FACTOR_RANK, QUERY_HEADS * HEAD_SIZE), FACTOR_RANK ** -0.5, 0.75, ((0, 2), (2, 2)))
    output_down_factors = gaussian(part_splits[9], (ADAPTER_TOTAL, FACTOR_RANK, QUERY_HEADS * HEAD_SIZE), (QUERY_HEADS * HEAD_SIZE) ** -0.5, 0.0625, ((0, 2), (2, 2)))
    output_up_factors = gaussian(part_splits[10], (ADAPTER_TOTAL, FACTOR_RANK, MODEL_WIDTH), FACTOR_RANK ** -0.5, 0.75, ((0, 2), (2, 2)))
    return dict(hidden=hidden, base_query_rows=base_query_rows, fresh_key_value=fresh_key_value, suffix_key_value=suffix_key_value, suffix_length=suffix_length, row_adapter_index=row_adapter_index, prompt_key_value=prompt_key_value, query_down_factors=query_down_factors, query_up_factors=query_up_factors, output_down_factors=output_down_factors, output_up_factors=output_up_factors)


rope_base = 1000000.0

def rotate(values_in, position):
    half_dim = values_in.shape[-1] // 2
    frequency = rope_base ** (-2.0 * jnp.arange(half_dim, dtype=jnp.float32) / values_in.shape[-1])
    angles = position[..., None] * frequency
    cos_part = jnp.cos(angles)
    sin_part = jnp.sin(angles)
    first_half = values_in[..., :half_dim]
    second_half = values_in[..., half_dim:]
    return jnp.concatenate([first_half * cos_part - second_half * sin_part, second_half * cos_part + first_half * sin_part], -1)

def rounded_values(values_in):
    narrow = lax.optimization_barrier(values_in.astype(jnp.bfloat16))
    return narrow.astype(jnp.float32)

def down_projected(inputs, factors, adapter_of_row):

    def add_adapter(carried, pair):
        factor, index = pair
        term = jnp.einsum('rsc,kc->rsk', inputs, factor.astype(jnp.float32))
        picked = (adapter_of_row == index)[:, None, None]
        return (carried + jnp.where(picked, term, 0.0), None)
    start = jnp.zeros(inputs.shape[:2] + (factors.shape[1],), jnp.float32)
    result, unused = lax.scan(add_adapter, start, (factors, jnp.arange(factors.shape[0], dtype=jnp.int32)))
    return result

def up_projected(inputs, factors, adapter_of_row):

    def add_adapter(carried, pair):
        factor, index = pair
        term = jnp.einsum('rsk,kc->rsc', inputs, factor.astype(jnp.float32))
        picked = (adapter_of_row == index)[:, None, None]
        return (carried + jnp.where(picked, term, 0.0), None)
    start = jnp.zeros(inputs.shape[:2] + (factors.shape[2],), jnp.float32)
    result, unused = lax.scan(add_adapter, start, (factors, jnp.arange(factors.shape[0], dtype=jnp.int32)))
    return result

def combine_parts(former, latter):
    weighted_a, peaks_a, totals_a = former
    weighted_b, peaks_b, totals_b = latter
    peaks = jnp.maximum(peaks_a, peaks_b)
    factor_a = jnp.exp(peaks_a - peaks)
    factor_b = jnp.exp(peaks_b - peaks)
    return (weighted_a * factor_a[..., None] + weighted_b * factor_b[..., None], peaks, totals_a * factor_a + totals_b * factor_b)

def reference(hidden, base_query_rows, fresh_key_value, suffix_key_value, suffix_length, row_adapter_index, prompt_key_value, query_down_factors, query_up_factors, output_down_factors, output_up_factors):
    adapter_of_row = row_adapter_index[:, 0]
    group_size = QUERY_HEADS // KVH
    score_scale = 1.0 / math.sqrt(HEAD_SIZE)
    query_low_rank = rounded_values(down_projected(hidden.astype(jnp.float32), query_down_factors, adapter_of_row))
    query_adjustment = up_projected(query_low_rank, query_up_factors, adapter_of_row)
    position = (PROMPT + suffix_length[:, None] + jnp.arange(STEPS, dtype=jnp.int32)[None, :]).astype(jnp.float32)
    merged = (base_query_rows.astype(jnp.float32) + query_adjustment).reshape(ROWS, STEPS, QUERY_HEADS, HEAD_SIZE)
    grouped = rounded_values(rotate(merged, position[:, :, None])).reshape(ROWS, STEPS, KVH, group_size, HEAD_SIZE)
    local_keys = jnp.concatenate([suffix_key_value[0], fresh_key_value[0]], 1).astype(jnp.float32).reshape(ROWS, SUF + STEPS, KVH, HEAD_SIZE)
    local_values = jnp.concatenate([suffix_key_value[1], fresh_key_value[1]], 1).astype(jnp.float32).reshape(ROWS, SUF + STEPS, KVH, HEAD_SIZE)
    scores = jnp.einsum('rtkgd,rpkd->rtkgp', grouped, local_keys) * score_scale
    key_slot = jnp.arange(SUF + STEPS, dtype=jnp.int32)[None, None, :]
    admitted = jnp.where(key_slot < SUF, key_slot < suffix_length[:, None, None], key_slot - SUF <= jnp.arange(STEPS, dtype=jnp.int32)[None, :, None])
    admitted = admitted[:, :, None, None, :]
    masked = jnp.where(admitted, scores, -1e+30)
    local_peaks = lax.optimization_barrier(jnp.max(masked, -1))
    local_weight = rounded_values(jnp.where(admitted, jnp.exp(masked - local_peaks[..., None]), 0.0))
    local_weighted = jnp.einsum('rtkgp,rpkd->rtkgd', local_weight, local_values)
    local_totals = lax.optimization_barrier(jnp.sum(local_weight, -1))
    token_count = ROWS * STEPS
    local_part = (local_weighted.reshape(token_count, KVH, group_size, HEAD_SIZE), local_peaks.reshape(token_count, KVH, group_size), local_totals.reshape(token_count, KVH, group_size))
    flat_query = grouped.reshape(token_count, KVH, group_size, HEAD_SIZE)
    prompt_keys = prompt_key_value[0].reshape(N_SEQ, P_DEV, KVH, HEAD_SIZE)
    prompt_values = prompt_key_value[1].reshape(N_SEQ, P_DEV, KVH, HEAD_SIZE)

    def add_block(carried, pair):
        block_keys, block_values = pair
        block_scores = jnp.einsum('nkgd,pkd->nkgp', flat_query, block_keys.astype(jnp.float32)) * score_scale
        peaks = lax.optimization_barrier(jnp.max(block_scores, -1))
        weight = rounded_values(jnp.exp(block_scores - peaks[..., None]))
        weighted = jnp.einsum('nkgp,pkd->nkgd', weight, block_values.astype(jnp.float32))
        totals = lax.optimization_barrier(jnp.sum(weight, -1))
        return (combine_parts(carried, (weighted, peaks, totals)), None)
    combined, unused = lax.scan(add_block, local_part, (prompt_keys, prompt_values))
    attended = (combined[0] / combined[2][..., None]).reshape(ROWS, STEPS, QUERY_HEADS * HEAD_SIZE).astype(jnp.bfloat16)
    attended_full_width = lax.optimization_barrier(attended).astype(jnp.float32)
    output_rank_rows = rounded_values(down_projected(attended_full_width, output_down_factors, adapter_of_row))
    adapted = up_projected(output_rank_rows, output_up_factors, adapter_of_row).astype(jnp.bfloat16)
    return (attended, adapted)
```

```python
import functools
import math

import jax
import jax.numpy as jnp
from jax import lax
from jax.experimental import pallas as pl
from jax.experimental.pallas import tpu as pltpu
from jax.sharding import PartitionSpec as P

HEAD_SIZE = 128
LANES = 128
rope_base = 1000000.0
MASKED = -1e30

VMEM = pl.BlockSpec(memory_space=pltpu.VMEM)
SMEM = pl.BlockSpec(memory_space=pltpu.SMEM)
F32 = jnp.float32
BF16 = jnp.bfloat16


def peer(index, offset, size):
    if size & (size - 1) == 0:
        return index ^ offset
    return (index + offset) % size


def fetch(value, axis, offset):
    size = lax.axis_size(axis)
    return lax.ppermute(value, axis, [(peer(i, offset, size), i) for i in range(size)])


def send(value, axis, offset):
    size = lax.axis_size(axis)
    return lax.ppermute(value, axis, [(i, peer(i, offset, size)) for i in range(size)])


def dot(left, right, contract):
    return lax.dot_general(left, right, (contract, ((), ())), preferred_element_type=F32)


def call(kernel, out_shape, args, specs=None, scratch=(), flops=1 << 20, vmem=24 << 20):
    return pl.pallas_call(
        kernel,
        out_shape=out_shape,
        in_specs=specs or [VMEM] * len(args),
        out_specs=jax.tree.map(lambda unused: VMEM, out_shape),
        scratch_shapes=scratch,
        compiler_params=pltpu.CompilerParams(vmem_limit_bytes=vmem),
        cost_estimate=pl.CostEstimate(flops=flops, bytes_accessed=1 << 20, transcendentals=0),
    )(*args)


def row_values(ref, rows, shape):
    row = lax.broadcasted_iota(jnp.int32, shape, 0) % rows
    out = jnp.zeros(shape, jnp.int32)
    for r in range(rows):
        out = jnp.where(row == r, ref[r], out)
    return out


def pack_kernel(base_ref, length_ref, id_ref, out_ref):
    steps, rows, width = base_ref.shape
    lane = lax.broadcasted_iota(jnp.int32, (rows, LANES), 1)
    lengths = row_values(length_ref, rows, (rows, LANES))
    ids = row_values(id_ref, rows, (rows, LANES))
    for t in range(steps):
        out_ref[t, :, :width] = base_ref[t]
        meta = jnp.where(lane == 0, lengths + t, jnp.where(lane == 1, ids, 0))
        out_ref[t, :, width:] = meta.astype(F32).astype(BF16)


def rank_kernel(adapters, *refs):
    hidden = refs[:adapters]
    down_ref, out_ref, gathered = refs[adapters:]
    steps, rows, width = hidden[0].shape
    pad_rows = out_ref.shape[3]
    resident, rank, _ = down_ref.shape
    gathered[...] = jnp.zeros_like(gathered)
    for j in range(adapters):
        for t in range(steps):
            at = j * pad_rows + t * rows
            gathered[at : at + rows, :] = hidden[j][t].astype(F32)
    result = dot(
        gathered[...].astype(BF16), down_ref[...].reshape(resident * rank, width), ((1,), (1,))
    )
    high = result.astype(BF16).astype(F32)
    low = result - high
    both = jnp.concatenate([high, low], axis=1).astype(BF16)
    me = lax.axis_index("adapter")
    for j in range(adapters):
        block = both[j * pad_rows : (j + 1) * pad_rows]
        target = peer(me, j, adapters)
        for s in range(out_ref.shape[0]):
            for h in range(out_ref.shape[2]):
                out_ref[s, target, h] = block


def rope_kernel(count, *refs):
    pieces = refs[:count]
    table_ref, out_ref, aux_ref = refs[count:]
    steps, rows, full = pieces[0].shape
    width = full - LANES
    tokens = out_ref.shape[0]
    for i in range(count):
        for t in range(steps):
            at = (i * steps + t) * rows
            out_ref[at : at + rows, :] = pieces[i][t, :, :width].astype(F32)
            aux_ref[at : at + rows, 2 * LANES :] = pieces[i][t, :, width:].astype(F32)
    meta = aux_ref[:, 2 * LANES :]
    slots = table_ref.shape[0]
    picked = lax.broadcasted_iota(jnp.int32, (tokens, slots), 1).astype(F32) == meta[:, 0:1]
    angles = lax.dot_general(
        picked.astype(F32),
        table_ref[...],
        (((1,), (0,)), ((), ())),
        precision=lax.Precision.HIGHEST,
        preferred_element_type=F32,
    )
    aux_ref[:, : 2 * LANES] = angles
    cos_part, sin_part = angles[:, :LANES], angles[:, LANES:]
    for h in range(width // HEAD_SIZE):
        at = pl.ds(h * HEAD_SIZE, HEAD_SIZE)
        piece = out_ref[:, at]
        out_ref[:, at] = piece * cos_part + pltpu.roll(piece, HEAD_SIZE // 2, 1) * sin_part


def attend(query, key, value, scale, extra=None):
    scores = dot(query, key, ((1,), (1,)))
    if extra is not None:
        more_key, more_value, bias = extra
        scores = jnp.concatenate([scores, dot(query, more_key, ((1,), (1,))) + bias], axis=1)
        value = jnp.concatenate([value, more_value], axis=0)
    peaks = jnp.max(scores, axis=1, keepdims=True)
    weight = jnp.exp2((scores - peaks) * scale).astype(BF16)
    ones = jnp.ones((value.shape[0], LANES), BF16)
    summed = dot(weight, jnp.concatenate([value, ones], axis=1), ((1,), (0,)))
    total = summed[:, HEAD_SIZE:]
    return summed[:, :HEAD_SIZE] / total, peaks * scale + jnp.log2(total)


def split_stat(stat, heads):
    first = stat.astype(BF16).astype(F32)
    second = (stat - first).astype(BF16).astype(F32)
    third = stat - first - second
    lane = lax.broadcasted_iota(jnp.int32, stat.shape, 1)
    out = jnp.where(lane < heads, first, 0.0)
    out = jnp.where((lane >= heads) & (lane < 2 * heads), pltpu.roll(second, heads, 1), out)
    out = jnp.where(
        (lane >= 2 * heads) & (lane < 3 * heads), pltpu.roll(third, 2 * heads, 1), out
    )
    return out


def store_messages(out_refs, kept, stats, steps, rows, heads):
    width = kept.shape[1]
    packed = split_stat(stats[...], heads)
    for i, ref in enumerate(out_refs):
        for t in range(steps):
            at = (i * steps + t) * rows
            ref[t, :, :width] = kept[at : at + rows, :].astype(BF16)
            ref[t, :, width:] = packed[at : at + rows, :].astype(BF16)


def far_kernel(order, split, adapters, scale, *refs):
    rope_ref, aux_ref, rank_ref = refs[:3]
    ups = refs[3 : 3 + adapters]
    kv_ref = refs[3 + adapters]
    out_refs = refs[4 + adapters : 4 + adapters + split]
    query_ref, ranks, kept, stats = refs[4 + adapters + split :]
    steps, rows, _ = out_refs[0].shape
    tokens = steps * rows
    seq_count, _, halves, pad_rows, double = rank_ref.shape
    depth = double // 2
    resident, rank, width = ups[0].shape
    heads = width // HEAD_SIZE
    kv_heads = kv_ref.shape[2] // HEAD_SIZE
    group = heads // kv_heads
    z, x = lax.axis_index("seq"), lax.axis_index("adapter")
    for i, k in enumerate(order):
        columns = []
        for j in range(adapters):
            total = jnp.zeros((pad_rows, double), F32)
            for h in range(halves):
                total += rank_ref[peer(z, k, seq_count), peer(x, j, adapters), h].astype(F32)
            columns.append(total[:, :depth] + total[:, depth:])
        ranks[i * tokens : (i + 1) * tokens, :] = jnp.concatenate(columns, axis=1)[:tokens]
    ids = aux_ref[:, 2 * LANES + 1 : 2 * LANES + 2]
    lane = lax.broadcasted_iota(jnp.int32, ranks.shape, 1)
    owner = (peer(x, lane // depth, adapters) * resident + lane % depth // rank).astype(F32)
    chosen = jnp.where(owner == ids, ranks[...], 0.0).astype(BF16)
    cos_part, sin_part = aux_ref[:, :LANES], aux_ref[:, LANES : 2 * LANES]
    cut = split * tokens
    lane = lax.broadcasted_iota(jnp.int32, (cut, LANES), 1)
    for kv in range(kv_heads):
        first = kv * group * HEAD_SIZE
        factors = jnp.concatenate(
            [up[u, :, first : first + group * HEAD_SIZE] for up in ups for u in range(resident)],
            axis=0,
        )
        delta = dot(chosen, factors, ((1,), (0,)))
        near, far = [], []
        for g in range(group):
            piece = delta[:, g * HEAD_SIZE : (g + 1) * HEAD_SIZE]
            turned = piece * cos_part + pltpu.roll(piece, HEAD_SIZE // 2, 1) * sin_part
            turned += rope_ref[:, first + g * HEAD_SIZE : first + (g + 1) * HEAD_SIZE]
            far.append(turned[:cut])
            near.append(turned[cut:])
        query_ref[kv] = jnp.concatenate(near, axis=0).astype(BF16)
        at = pl.ds(kv * HEAD_SIZE, HEAD_SIZE)
        result, level = attend(
            jnp.concatenate(far, axis=0).astype(BF16), kv_ref[0, :, at], kv_ref[1, :, at], scale
        )
        for g in range(group):
            head = kv * group + g
            kept[:, head * HEAD_SIZE : (head + 1) * HEAD_SIZE] = result[g * cut : (g + 1) * cut]
            piece = level[g * cut : (g + 1) * cut]
            stats[...] = jnp.where(lane == head, piece, stats[...] if head else 0.0)
    store_messages(out_refs, kept, stats, steps, rows, heads)


def near_kernel(split, scale, *refs):
    query_ref, kv_ref, suffix_ref, fresh_ref, length_ref = refs[:5]
    out_refs = refs[5 : 5 + split - 1]
    own_ref, level_ref, kept, stats, fresh_rows = refs[5 + split - 1 :]
    _, steps, rows, _ = fresh_ref.shape
    slots = suffix_ref.shape[2]
    width = kept.shape[1]
    heads = width // HEAD_SIZE
    kv_heads = kv_ref.shape[2] // HEAD_SIZE
    group = heads // kv_heads
    tokens = steps * rows
    cut = split * tokens
    fresh_slots = fresh_rows.shape[1]
    fresh_rows[...] = jnp.zeros_like(fresh_rows)
    for part in range(2):
        for t in range(steps):
            fresh_rows[part, t * rows : (t + 1) * rows, :] = fresh_ref[part, t].astype(F32)
    suffix_count = rows * slots
    shape = (cut, suffix_count + fresh_slots)
    token = lax.broadcasted_iota(jnp.int32, shape, 0)
    column = lax.broadcasted_iota(jnp.int32, shape, 1)
    token_row, token_step = token % rows, token // rows
    fresh_at = column - suffix_count
    in_suffix = (column < suffix_count) & (column // slots == token_row)
    in_suffix &= column % slots < row_values(length_ref, rows, shape)
    in_fresh = (column >= suffix_count) & (fresh_at % rows == token_row)
    in_fresh &= fresh_at // rows <= token_step
    bias = jnp.where((in_suffix | in_fresh) & (token < tokens), 0.0, MASKED)
    bias = jnp.concatenate([bias] * group, axis=0)
    lane = lax.broadcasted_iota(jnp.int32, (cut, LANES), 1)
    for kv in range(kv_heads):
        at = pl.ds(kv * HEAD_SIZE, HEAD_SIZE)
        more = [
            jnp.concatenate(
                [suffix_ref[part, r, :, at] for r in range(rows)]
                + [fresh_rows[part, :, at].astype(BF16)],
                axis=0,
            )
            for part in range(2)
        ]
        result, level = attend(
            query_ref[kv], kv_ref[0, :, at], kv_ref[1, :, at], scale, (more[0], more[1], bias)
        )
        for g in range(group):
            head = kv * group + g
            kept[:, head * HEAD_SIZE : (head + 1) * HEAD_SIZE] = result[g * cut : (g + 1) * cut]
            piece = level[g * cut : (g + 1) * cut]
            stats[...] = jnp.where(lane == head, piece, stats[...] if head else 0.0)
    for t in range(steps):
        own_ref[t] = kept[t * rows : (t + 1) * rows, :]
        level_ref[t] = stats[t * rows : (t + 1) * rows, :]
    packed = split_stat(stats[...], heads)
    for i, ref in enumerate(out_refs):
        for t in range(steps):
            at = ((i + 1) * steps + t) * rows
            ref[t, :, :width] = kept[at : at + rows, :].astype(BF16)
            ref[t, :, width:] = packed[at : at + rows, :].astype(BF16)


def merge_kernel(messages, adapters, *refs):
    own_ref, level_ref = refs[:2]
    arrived = refs[2 : 2 + messages]
    downs = refs[2 + messages : 2 + messages + adapters]
    id_ref, out_ref, rank_ref, rows_ref = refs[2 + messages + adapters :]
    steps, rows, width = own_ref.shape
    heads = width // HEAD_SIZE
    resident, rank, _ = downs[0].shape
    depth = resident * rank
    x = lax.axis_index("adapter")
    rows_ref[...] = jnp.zeros_like(rows_ref)
    for t in range(steps):
        levels = [level_ref[t]]
        for ref in arrived:
            packed = ref[t, :, width:].astype(F32)
            count = packed.shape[1]
            levels.append(
                packed
                + pltpu.roll(packed, count - heads, 1)
                + pltpu.roll(packed, count - 2 * heads, 1)
            )
        highest = functools.reduce(jnp.maximum, levels)
        shares = [jnp.exp2(level - highest) for level in levels]
        total = functools.reduce(jnp.add, shares)
        shares = [share / total for share in shares]
        for h in range(heads):
            at = pl.ds(h * HEAD_SIZE, HEAD_SIZE)
            mixed = own_ref[t, :, at] * shares[0][:, h : h + 1]
            for ref, share in zip(arrived, shares[1:]):
                mixed += ref[t, :, at].astype(F32) * share[:, h : h + 1]
            out_ref[t, :, at] = mixed.astype(BF16)
            rows_ref[t * rows : (t + 1) * rows, at] = mixed
    factors = jnp.concatenate([down[u] for down in downs for u in range(resident)], axis=0)
    result = dot(rows_ref[...].astype(BF16), factors, ((1,), (1,)))
    ids = row_values(id_ref, rows, result.shape)
    lane = lax.broadcasted_iota(jnp.int32, result.shape, 1)
    owner = peer(x, lane // depth, adapters) * resident + lane % depth // rank
    rank_ref[...] = jnp.where(owner == ids, result, 0.0)


def up_kernel(parts, adapters, *refs):
    ranks = refs[:parts]
    ups = refs[parts : parts + adapters]
    out_ref = refs[parts + adapters]
    steps, rows, width = out_ref.shape
    resident = ups[0].shape[0]
    chosen = functools.reduce(jnp.add, [ref[...] for ref in ranks]).astype(BF16)
    factors = jnp.concatenate([up[u] for up in ups for u in range(resident)], axis=0)
    result = dot(chosen, factors, ((1,), (0,)))
    for t in range(steps):
        out_ref[t] = result[t * rows : (t + 1) * rows].astype(BF16)


def rope_table(slots, first_position):
    half_dim = HEAD_SIZE // 2
    frequency = rope_base ** (-2.0 * jnp.arange(half_dim, dtype=F32) / HEAD_SIZE)
    position = (first_position + jnp.arange(slots, dtype=jnp.int32)).astype(F32)
    angles = position[:, None] * frequency
    cos_part, sin_part = jnp.cos(angles), jnp.sin(angles)
    return jnp.concatenate([cos_part, cos_part, -sin_part, sin_part], axis=1)


def on_device(
    hidden,
    base_query_rows,
    fresh_key_value,
    suffix_key_value,
    suffix_length,
    row_adapter_index,
    prompt_key_value,
    query_down_factors,
    query_up_factors,
    output_down_factors,
    output_up_factors,
):
    rows, steps, width = hidden.shape
    seq_count, adapters, halves = (lax.axis_size(name) for name in ("seq", "adapter", "head"))
    slots = suffix_key_value.shape[2]
    resident, rank, _ = query_down_factors.shape
    depth = resident * rank
    tokens = rows * steps
    pad_rows = -(-tokens // 16) * 16
    heads = width // HEAD_SIZE
    kv_heads = prompt_key_value.shape[2] // HEAD_SIZE
    group = heads // kv_heads
    scale = math.log2(math.e) / math.sqrt(HEAD_SIZE)
    stat_lanes = -(-3 * heads // LANES) * LANES
    ids = row_adapter_index.reshape(-1)
    hidden = hidden.transpose(1, 0, 2)
    base = base_query_rows.transpose(1, 0, 2)
    fresh = fresh_key_value.transpose(0, 2, 1, 3)

    hidden_of = [hidden] + [fetch(hidden, "adapter", j) for j in range(1, adapters)]
    query_ups = [query_up_factors] + [
        fetch(query_up_factors, "adapter", j) for j in range(1, adapters)
    ]
    packed = call(
        pack_kernel,
        jax.ShapeDtypeStruct((steps, rows, width + LANES), BF16),
        (base, suffix_length, ids),
        [VMEM, SMEM, SMEM],
    )
    split = seq_count // 2
    order = list(range(seq_count - 1, split - 1, -1)) + list(range(split))
    pieces = [fetch(packed, "seq", k) if k else packed for k in order]
    table_slots = -(-(slots + steps) // 8) * 8
    table = rope_table(table_slots, prompt_key_value.shape[1] * seq_count)
    roped, aux = call(
        functools.partial(rope_kernel, seq_count),
        (
            jax.ShapeDtypeStruct((seq_count * tokens, width), F32),
            jax.ShapeDtypeStruct((seq_count * tokens, 3 * LANES), F32),
        ),
        (*pieces, table),
        flops=1 << 34,
    )
    rank_parts = call(
        functools.partial(rank_kernel, adapters),
        jax.ShapeDtypeStruct((seq_count, adapters, halves, pad_rows, 2 * depth), BF16),
        (*hidden_of, query_down_factors),
        scratch=[pltpu.VMEM((adapters * pad_rows, width), F32)],
    )
    spread = (seq_count * adapters * halves,) + rank_parts.shape[3:]
    rank_parts = lax.all_to_all(
        rank_parts.reshape(spread),
        ("seq", "adapter", "head"),
        split_axis=0,
        concat_axis=0,
        tiled=True,
    ).reshape(rank_parts.shape)

    message = jax.ShapeDtypeStruct((steps, rows, width + stat_lanes), BF16)
    *far_messages, near_query = call(
        functools.partial(far_kernel, order, seq_count - split, adapters, scale),
        (message,) * (seq_count - split)
        + (jax.ShapeDtypeStruct((kv_heads, group * split * tokens, HEAD_SIZE), BF16),),
        (roped, aux, rank_parts, *query_ups, prompt_key_value),
        scratch=[
            pltpu.VMEM((seq_count * tokens, adapters * depth), F32),
            pltpu.VMEM(((seq_count - split) * tokens, width), F32),
            pltpu.VMEM(((seq_count - split) * tokens, LANES), F32),
        ],
    )
    output_downs = [output_down_factors] + [
        fetch(output_down_factors, "adapter", j) for j in range(1, adapters)
    ]
    output_ups = [output_up_factors] + [
        fetch(output_up_factors, "adapter", j) for j in range(1, adapters)
    ]
    arrived = [send(part, "seq", k) for part, k in zip(far_messages, order)]
    fresh_slots = -(-tokens // LANES) * LANES
    *near_messages, own, level = call(
        functools.partial(near_kernel, split, scale),
        (message,) * (split - 1)
        + (
            jax.ShapeDtypeStruct((steps, rows, width), F32),
            jax.ShapeDtypeStruct((steps, rows, LANES), F32),
        ),
        (near_query, prompt_key_value, suffix_key_value, fresh, suffix_length),
        [VMEM] * 4 + [SMEM],
        scratch=[
            pltpu.VMEM((split * tokens, width), F32),
            pltpu.VMEM((split * tokens, LANES), F32),
            pltpu.VMEM((2, fresh_slots, fresh.shape[3]), F32),
        ],
    )
    arrived += [send(part, "seq", k) for part, k in zip(near_messages, order[seq_count - split + 1 :])]
    attended, out_rank = call(
        functools.partial(merge_kernel, seq_count - 1, adapters),
        (
            jax.ShapeDtypeStruct((steps, rows, width), BF16),
            jax.ShapeDtypeStruct((pad_rows, adapters * depth), F32),
        ),
        (own, level, *arrived, *output_downs, ids),
        [VMEM] * (2 + len(arrived) + adapters) + [SMEM],
        scratch=[pltpu.VMEM((pad_rows, width), F32)],
    )
    out_ranks = [out_rank] + [fetch(out_rank, "head", j) for j in range(1, halves)]
    adapted = call(
        functools.partial(up_kernel, halves, adapters),
        jax.ShapeDtypeStruct((steps, rows, width), BF16),
        (*out_ranks, *output_ups),
    )
    return attended.transpose(1, 0, 2), adapted.transpose(1, 0, 2)


def solution(mesh):
    rows = ("groups", "seq", "adapter")
    factors = P(("groups", "adapter"), None, "head")
    placed = (
        P(rows, None, "head"),
        P(rows, None, "head"),
        P(None, rows, None, "head"),
        P(None, rows, None, "head"),
        P(rows),
        P(rows, None),
        P(None, ("groups", "seq"), "head"),
        factors,
        factors,
        factors,
        factors,
    )
    return jax.shard_map(
        on_device,
        mesh=mesh,
        in_specs=placed,
        out_specs=(P(rows, None, "head"), P(rows, None, "head")),
        check_vma=False,
    )
```

```python
import functools
import math

import jax
import jax.numpy as jnp
from jax import lax
from jax.experimental import pallas as pl
from jax.experimental.pallas import tpu as pltpu
from jax.sharding import PartitionSpec as P

HEAD_SIZE = 128
LANES = 128
rope_base = 1000000.0
MASKED = -1e30
VMEM_BYTES = 8 << 20

VMEM = pl.BlockSpec(memory_space=pltpu.VMEM)
SMEM = pl.BlockSpec(memory_space=pltpu.SMEM)
F32 = jnp.float32
BF16 = jnp.bfloat16


def peer(index, offset, size):
    if size & (size - 1) == 0:
        return index ^ offset
    return (index + offset) % size


def fetch(value, axis, offset):
    size = lax.axis_size(axis)
    return lax.ppermute(value, axis, [(peer(i, offset, size), i) for i in range(size)])


def send(value, axis, offset):
    size = lax.axis_size(axis)
    return lax.ppermute(value, axis, [(i, peer(i, offset, size)) for i in range(size)])


def dot(left, right, contract):
    return lax.dot_general(left, right, (contract, ((), ())), preferred_element_type=F32)


def call(kernel, out_shape, args, specs=None, scratch=(), flops=1 << 20, out_specs=None):
    return pl.pallas_call(
        kernel,
        out_shape=out_shape,
        in_specs=specs or [VMEM] * len(args),
        out_specs=out_specs or jax.tree.map(lambda unused: VMEM, out_shape),
        scratch_shapes=scratch,
        compiler_params=pltpu.CompilerParams(vmem_limit_bytes=VMEM_BYTES),
        cost_estimate=pl.CostEstimate(flops=flops, bytes_accessed=1 << 20, transcendentals=0),
    )(*args)


def row_values(ref, rows, shape):
    row = lax.broadcasted_iota(jnp.int32, shape, 0) % rows
    out = jnp.zeros(shape, jnp.int32)
    for r in range(rows):
        out = jnp.where(row == r, ref[r], out)
    return out


def rank_kernel(count, *refs):
    parts = refs[:count]
    down_ref = refs[count]
    earlier = refs[count + 1 : -3]
    out_ref, kept_ref, gathered = refs[-3:]
    kept_ref[...] = down_ref[...]
    steps, rows, width = parts[0].shape
    resident, rank, _ = down_ref.shape
    pad_rows = gathered.shape[0] // count
    for j, ref in enumerate(parts):
        for t in range(steps):
            at = j * pad_rows + t * rows
            gathered[at : at + rows, :] = ref[t].astype(F32)
        at = j * pad_rows + steps * rows
        gathered[at : (j + 1) * pad_rows, :] = jnp.zeros((pad_rows - steps * rows, width), F32)
    result = dot(
        gathered[...].astype(BF16), down_ref[...].reshape(resident * rank, width), ((1,), (1,))
    )
    for ref in earlier:
        out_ref[: ref.shape[0], :] = ref[...]
    out_ref[out_ref.shape[0] - result.shape[0] :, :] = result


def correction_kernel(parts, *refs):
    ranks = functools.reduce(jnp.add, [ref[...] for ref in refs[:parts]]).astype(BF16)
    up_ref = refs[parts]
    out_refs = refs[parts + 1 :]
    resident, rank, _ = up_ref.shape
    _, steps, rows, _ = out_refs[0].shape
    pad_rows = ranks.shape[0] // len(out_refs)
    for u in range(resident):
        result = dot(ranks[:, u * rank : (u + 1) * rank], up_ref[u], ((1,), (0,)))
        for j, ref in enumerate(out_refs):
            for t in range(steps):
                at = j * pad_rows + t * rows
                ref[u, t] = result[at : at + rows]


def copy_kernel(in_ref, out_ref):
    out_ref[...] = in_ref[...]


def prepare_kernel(correction_ref, base_ref, suffix_ref, fresh_ref, length_ref, id_ref, *refs):
    sum_ref, id_rows_ref, suffix_out, fresh_out, bias_ref, token_ref = refs
    resident, steps, rows, width = correction_ref.shape
    x = lax.axis_index("adapter")
    ids = row_values(id_ref, rows, (rows, LANES))
    id_rows_ref[...] = ids
    for t in range(steps):
        for h in range(width // HEAD_SIZE):
            at = pl.ds(h * HEAD_SIZE, HEAD_SIZE)
            piece = base_ref[t, :, at].astype(F32)
            for u in range(resident):
                piece += jnp.where(ids == x * resident + u, correction_ref[u, t, :, at], 0.0)
            sum_ref[t, :, at] = piece
    suffix_out[...] = suffix_ref[...]
    fresh_out[...] = jnp.zeros_like(fresh_out)
    for part in range(2):
        for t in range(steps):
            fresh_out[part, t * rows : (t + 1) * rows, :] = fresh_ref[part, t].astype(F32)
    slots = suffix_ref.shape[2]
    suffix_count = rows * slots
    shape = bias_ref.shape
    token = lax.broadcasted_iota(jnp.int32, shape, 0)
    column = lax.broadcasted_iota(jnp.int32, shape, 1)
    token_row, token_step = token % rows, token // rows
    fresh_at = column - suffix_count
    in_suffix = (column < suffix_count) & (column // slots == token_row)
    in_suffix &= column % slots < row_values(length_ref, rows, shape)
    in_fresh = (column >= suffix_count) & (fresh_at % rows == token_row)
    in_fresh &= fresh_at // rows <= token_step
    bias_ref[...] = jnp.where(in_suffix | in_fresh, 0.0, MASKED)
    token_ref[...] = jnp.zeros_like(token_ref)


def rotate_kernel(others, *refs):
    corrections = refs[:others]
    sum_ref, cos_ref, sin_ref, id_ref, _, out_ref = refs[others:]
    steps, rows, width = sum_ref.shape
    x = lax.axis_index("adapter")
    ids = id_ref[...]
    for t in range(steps):
        cos_part, sin_part = cos_ref[t], sin_ref[t]
        for h in range(width // HEAD_SIZE):
            at = pl.ds(h * HEAD_SIZE, HEAD_SIZE)
            piece = sum_ref[t, :, at]
            for j, ref in enumerate(corrections):
                resident = ref.shape[0]
                for u in range(resident):
                    owner = peer(x, j + 1, others + 1) * resident + u
                    piece += jnp.where(ids == owner, ref[u, t, :, at], 0.0)
            turned = piece * cos_part + pltpu.roll(piece, HEAD_SIZE // 2, 1) * sin_part
            out_ref[t, :, at] = turned.astype(BF16)


def load_queries(query_ref, rows_ref):
    steps, rows, _ = query_ref.shape
    rows_ref[...] = jnp.zeros_like(rows_ref)
    for t in range(steps):
        rows_ref[t * rows : (t + 1) * rows, :] = query_ref[t].astype(F32)


def group_queries(rows_ref, first, group):
    pieces = [
        rows_ref[:, first + g * HEAD_SIZE : first + (g + 1) * HEAD_SIZE] for g in range(group)
    ]
    return jnp.concatenate(pieces, axis=0).astype(BF16)


def attend(query, key, value, scale, extra=None):
    scores = dot(query, key, ((1,), (1,)))
    if extra is not None:
        more_key, more_value, bias = extra
        scores = jnp.concatenate([scores, dot(query, more_key, ((1,), (1,))) + bias], axis=1)
        value = jnp.concatenate([value, more_value], axis=0)
    peaks = jnp.max(scores, axis=1, keepdims=True)
    weight = jnp.exp2((scores - peaks) * scale).astype(BF16)
    ones = jnp.ones((value.shape[0], LANES), BF16)
    summed = dot(weight, jnp.concatenate([value, ones], axis=1), ((1,), (0,)))
    total = summed[:, HEAD_SIZE:]
    return summed[:, :HEAD_SIZE] / total, peaks * scale + jnp.log2(total)


def split_stat(stat, heads):
    first = stat.astype(BF16).astype(F32)
    second = (stat - first).astype(BF16).astype(F32)
    third = stat - first - second
    lane = lax.broadcasted_iota(jnp.int32, stat.shape, 1)
    out = jnp.where(lane < heads, first, 0.0)
    out = jnp.where((lane >= heads) & (lane < 2 * heads), pltpu.roll(second, heads, 1), out)
    out = jnp.where(
        (lane >= 2 * heads) & (lane < 3 * heads), pltpu.roll(third, 2 * heads, 1), out
    )
    return out


def far_kernel(scale, query_ref, kv_ref, *refs):
    out_ref, rows_ref, kept, stats = refs[-4:]
    steps, rows, width = query_ref.shape
    heads = width // HEAD_SIZE
    kv_heads = kv_ref.shape[2] // HEAD_SIZE
    group = heads // kv_heads
    cut = rows_ref.shape[0]
    load_queries(query_ref, rows_ref)
    lane = lax.broadcasted_iota(jnp.int32, (cut, LANES), 1)
    for kv in range(kv_heads):
        at = pl.ds(kv * HEAD_SIZE, HEAD_SIZE)
        queries = group_queries(rows_ref, kv * group * HEAD_SIZE, group)
        result, level = attend(queries, kv_ref[0, :, at], kv_ref[1, :, at], scale)
        for g in range(group):
            head = kv * group + g
            kept[:, head * HEAD_SIZE : (head + 1) * HEAD_SIZE] = result[g * cut : (g + 1) * cut]
            piece = level[g * cut : (g + 1) * cut]
            stats[...] = jnp.where(lane == head, piece, stats[...] if head else 0.0)
    packed = split_stat(stats[...], heads)
    for t in range(steps):
        at = t * rows
        out_ref[t, :, :width] = kept[at : at + rows, :].astype(BF16)
        out_ref[t, :, width:] = packed[at : at + rows, :].astype(BF16)


def near_kernel(scale, query_ref, kv_ref, suffix_ref, fresh_ref, bias_ref, *refs):
    own_ref, level_ref, token_ref, rows_ref, kept, stats = refs
    load_queries(query_ref, rows_ref)
    token_ref[...] = jnp.zeros_like(token_ref)
    steps, rows, width = query_ref.shape
    heads = width // HEAD_SIZE
    kv_heads = kv_ref.shape[2] // HEAD_SIZE
    group = heads // kv_heads
    cut = rows_ref.shape[0]
    bias = jnp.concatenate([bias_ref[...]] * group, axis=0)
    lane = lax.broadcasted_iota(jnp.int32, (cut, LANES), 1)
    for kv in range(kv_heads):
        at = pl.ds(kv * HEAD_SIZE, HEAD_SIZE)
        more = [
            jnp.concatenate(
                [suffix_ref[part, r, :, at] for r in range(rows)]
                + [fresh_ref[part, :, at].astype(BF16)],
                axis=0,
            )
            for part in range(2)
        ]
        result, level = attend(
            group_queries(rows_ref, kv * group * HEAD_SIZE, group),
            kv_ref[0, :, at],
            kv_ref[1, :, at],
            scale,
            (more[0], more[1], bias),
        )
        for g in range(group):
            head = kv * group + g
            kept[:, head * HEAD_SIZE : (head + 1) * HEAD_SIZE] = result[g * cut : (g + 1) * cut]
            piece = level[g * cut : (g + 1) * cut]
            stats[...] = jnp.where(lane == head, piece, stats[...] if head else 0.0)
    for t in range(steps):
        own_ref[t] = kept[t * rows : (t + 1) * rows, :]
        level_ref[t] = stats[t * rows : (t + 1) * rows, :]


def merge_kernel(messages, adapters, *refs):
    arrived = refs[:messages]
    own_ref, level_ref = refs[messages : messages + 2]
    downs = refs[2 + messages : 2 + messages + adapters]
    id_ref, out_hbm, rank_ref, rows_ref, out_ref, sem = refs[2 + messages + adapters :]
    steps, rows, width = own_ref.shape
    heads = width // HEAD_SIZE
    resident, rank, _ = downs[0].shape
    depth = resident * rank
    x = lax.axis_index("adapter")
    rows_ref[...] = jnp.zeros_like(rows_ref)
    for t in range(steps):
        levels = [level_ref[t]]
        for ref in arrived:
            packed = ref[t, :, width:].astype(F32)
            count = packed.shape[1]
            levels.append(
                packed
                + pltpu.roll(packed, count - heads, 1)
                + pltpu.roll(packed, count - 2 * heads, 1)
            )
        highest = functools.reduce(jnp.maximum, levels)
        shares = [jnp.exp2(level - highest) for level in levels]
        total = functools.reduce(jnp.add, shares)
        shares = [share / total for share in shares]
        for h in range(heads):
            at = pl.ds(h * HEAD_SIZE, HEAD_SIZE)
            mixed = own_ref[t, :, at] * shares[0][:, h : h + 1]
            for ref, share in zip(arrived, shares[1:]):
                mixed += ref[t, :, at].astype(F32) * share[:, h : h + 1]
            out_ref[t, :, at] = mixed.astype(BF16)
            rows_ref[t * rows : (t + 1) * rows, at] = mixed
    copy = pltpu.make_async_copy(out_ref, out_hbm, sem)
    copy.start()
    factors = jnp.concatenate([down[u] for down in downs for u in range(resident)], axis=0)
    result = dot(rows_ref[...].astype(BF16), factors, ((1,), (1,)))
    ids = row_values(id_ref, rows, result.shape)
    lane = lax.broadcasted_iota(jnp.int32, result.shape, 1)
    owner = peer(x, lane // depth, adapters) * resident + lane % depth // rank
    rank_ref[...] = jnp.where(owner == ids, result, 0.0)
    copy.wait()


def up_kernel(parts, adapters, *refs):
    ranks = refs[:parts]
    ups = refs[parts : parts + adapters]
    out_ref = refs[parts + adapters]
    steps, rows, width = out_ref.shape
    resident = ups[0].shape[0]
    chosen = functools.reduce(jnp.add, [ref[...] for ref in ranks]).astype(BF16)
    factors = jnp.concatenate([up[u] for up in ups for u in range(resident)], axis=0)
    result = dot(chosen, factors, ((1,), (0,)))
    for t in range(steps):
        out_ref[t] = result[t * rows : (t + 1) * rows].astype(BF16)


def rope_parts(suffix_length, steps, first_position):
    half_dim = HEAD_SIZE // 2
    frequency = rope_base ** (-2.0 * jnp.arange(half_dim, dtype=F32) / HEAD_SIZE)
    position = first_position + suffix_length[None, :] + jnp.arange(steps, dtype=jnp.int32)[:, None]
    angles = position.astype(F32)[..., None] * frequency
    cos_part, sin_part = jnp.cos(angles), jnp.sin(angles)
    return (
        jnp.concatenate([cos_part, cos_part], axis=-1),
        jnp.concatenate([-sin_part, sin_part], axis=-1),
    )


def on_device(
    hidden,
    base_query_rows,
    fresh_key_value,
    suffix_key_value,
    suffix_length,
    row_adapter_index,
    prompt_key_value,
    query_down_factors,
    query_up_factors,
    output_down_factors,
    output_up_factors,
):
    rows, steps, width = hidden.shape
    seq_count, adapters, halves = (lax.axis_size(name) for name in ("seq", "adapter", "head"))
    slots = suffix_key_value.shape[2]
    resident, rank, _ = query_down_factors.shape
    depth = resident * rank
    tokens = rows * steps
    pad_rows = -(-tokens // 16) * 16
    heads = width // HEAD_SIZE
    kv_heads = prompt_key_value.shape[2] // HEAD_SIZE
    group = heads // kv_heads
    scale = math.log2(math.e) / math.sqrt(HEAD_SIZE)
    stat_lanes = -(-3 * heads // LANES) * LANES
    ids = row_adapter_index.reshape(-1)
    hidden = hidden.transpose(1, 0, 2)
    base = base_query_rows.transpose(1, 0, 2)
    fresh = fresh_key_value.transpose(0, 2, 1, 3)

    own_rows = jax.ShapeDtypeStruct((pad_rows, depth), F32)
    factors = jax.ShapeDtypeStruct(query_down_factors.shape, BF16)
    own_ranks, own_down = call(
        functools.partial(rank_kernel, 1),
        (own_rows, factors),
        (hidden, query_down_factors),
        scratch=[pltpu.VMEM((pad_rows, width), F32)],
    )
    hidden_of = [fetch(hidden, "adapter", j) for j in range(1, adapters)]
    ranks, _ = call(
        functools.partial(rank_kernel, adapters - 1),
        (jax.ShapeDtypeStruct((adapters * pad_rows, depth), F32), factors),
        (*hidden_of, own_down, own_ranks),
        scratch=[pltpu.VMEM(((adapters - 1) * pad_rows, width), F32)],
    )
    rank_parts = [ranks] + [fetch(ranks, "head", j) for j in range(1, halves)]
    own_up = call(
        copy_kernel, jax.ShapeDtypeStruct(query_up_factors.shape, BF16), (query_up_factors,)
    )
    corrections = call(
        functools.partial(correction_kernel, halves),
        (jax.ShapeDtypeStruct((resident, steps, rows, width), F32),) * adapters,
        (*rank_parts, own_up),
    )
    arrived = [send(part, "adapter", j) for j, part in enumerate(corrections) if j]
    cos_part, sin_part = rope_parts(suffix_length, steps, prompt_key_value.shape[1] * seq_count)
    fresh_slots = -(-tokens // LANES) * LANES
    token_shape = jax.ShapeDtypeStruct((8, LANES), F32)
    query_sum, id_rows, suffix, fresh, bias, token = call(
        prepare_kernel,
        (
            jax.ShapeDtypeStruct((steps, rows, width), F32),
            jax.ShapeDtypeStruct((rows, LANES), jnp.int32),
            jax.ShapeDtypeStruct(suffix_key_value.shape, BF16),
            jax.ShapeDtypeStruct((2, fresh_slots, fresh.shape[3]), F32),
            jax.ShapeDtypeStruct((pad_rows, rows * slots + fresh_slots), F32),
            token_shape,
        ),
        (corrections[0], base, suffix_key_value, fresh, suffix_length, ids),
        [VMEM] * 4 + [SMEM] * 2,
    )
    output_down_factors, output_up_factors, token = lax.optimization_barrier(
        (output_down_factors, output_up_factors, token)
    )
    queries = call(
        functools.partial(rotate_kernel, adapters - 1),
        jax.ShapeDtypeStruct((steps, rows, width), BF16),
        (*arrived, query_sum, cos_part, sin_part, id_rows, token),
    )
    order = list(range(seq_count - 1, 0, -1))
    message = jax.ShapeDtypeStruct((steps, rows, width + stat_lanes), BF16)
    query_scratch = [
        pltpu.VMEM((pad_rows, width), F32),
        pltpu.VMEM((pad_rows, width), F32),
        pltpu.VMEM((pad_rows, LANES), F32),
    ]
    pieces = [fetch(queries, "seq", k) for k in order]
    own, level, token = call(
        functools.partial(near_kernel, scale),
        (
            jax.ShapeDtypeStruct((steps, rows, width), F32),
            jax.ShapeDtypeStruct((steps, rows, LANES), F32),
            token_shape,
        ),
        (queries, prompt_key_value, suffix, fresh, bias),
        scratch=query_scratch,
    )
    messages = [
        call(
            functools.partial(far_kernel, scale),
            message,
            (piece, prompt_key_value) + ((token,) if i == 0 else ()),
            scratch=query_scratch,
        )
        for i, piece in enumerate(pieces)
    ]
    output_downs = [output_down_factors] + [
        fetch(output_down_factors, "adapter", j) for j in range(1, adapters)
    ]
    output_ups = [output_up_factors] + [
        fetch(output_up_factors, "adapter", j) for j in range(1, adapters)
    ]
    partials = [send(part, "seq", k) for part, k in zip(messages, order)]
    attended, out_rank = call(
        functools.partial(merge_kernel, seq_count - 1, adapters),
        (
            jax.ShapeDtypeStruct((steps, rows, width), BF16),
            jax.ShapeDtypeStruct((pad_rows, adapters * depth), F32),
        ),
        (*partials, own, level, *output_downs, ids),
        [VMEM] * (2 + len(partials) + adapters) + [SMEM],
        scratch=[
            pltpu.VMEM((pad_rows, width), F32),
            pltpu.VMEM((steps, rows, width), BF16),
            pltpu.SemaphoreType.DMA,
        ],
        out_specs=(pl.BlockSpec(memory_space=pl.ANY), VMEM),
    )
    out_ranks = [out_rank] + [fetch(out_rank, "head", j) for j in range(1, halves)]
    adapted = call(
        functools.partial(up_kernel, halves, adapters),
        jax.ShapeDtypeStruct((steps, rows, width), BF16),
        (*out_ranks, *output_ups),
    )
    return attended.transpose(1, 0, 2), adapted.transpose(1, 0, 2)


def solution(mesh):
    rows = ("groups", "seq", "adapter")
    factors = P(("groups", "adapter"), None, "head")
    placed = (
        P(rows, None, "head"),
        P(rows, None, "head"),
        P(None, rows, None, "head"),
        P(None, rows, None, "head"),
        P(rows),
        P(rows, None),
        P(None, ("groups", "seq"), "head"),
        factors,
        factors,
        factors,
        factors,
    )
    return jax.shard_map(
        on_device,
        mesh=mesh,
        in_specs=placed,
        out_specs=(P(rows, None, "head"), P(rows, None, "head")),
        check_vma=False,
    )
```

```python
import functools
import math

import jax
import jax.numpy as jnp
from jax import lax
from jax.experimental import pallas as pl
from jax.experimental.pallas import tpu as pltpu
from jax.sharding import PartitionSpec as P

HEAD_SIZE = 128
LANES = 128
rope_base = 1000000.0
MASKED = -1e30
VMEM_BYTES = 8 << 20

VMEM = pl.BlockSpec(memory_space=pltpu.VMEM)
F32 = jnp.float32
BF16 = jnp.bfloat16


def peer(index, offset, size):
    if size & (size - 1) == 0:
        return index ^ offset
    return (index + offset) % size


def fetch(value, axis, offset):
    size = lax.axis_size(axis)
    return lax.ppermute(value, axis, [(peer(i, offset, size), i) for i in range(size)])


def send(value, axis, offset):
    size = lax.axis_size(axis)
    return lax.ppermute(value, axis, [(i, peer(i, offset, size)) for i in range(size)])


def dot(left, right, contract):
    return lax.dot_general(left, right, (contract, ((), ())), preferred_element_type=F32)


def call(kernel, out_shape, args, specs=None, scratch=(), flops=1 << 20, out_specs=None):
    return pl.pallas_call(
        kernel,
        out_shape=out_shape,
        in_specs=specs or [VMEM] * len(args),
        out_specs=out_specs or jax.tree.map(lambda unused: VMEM, out_shape),
        scratch_shapes=scratch,
        compiler_params=pltpu.CompilerParams(vmem_limit_bytes=VMEM_BYTES),
        cost_estimate=pl.CostEstimate(flops=flops, bytes_accessed=1 << 20, transcendentals=0),
    )(*args)


def rank_kernel(count, *refs):
    parts = refs[:count]
    down_ref = refs[count]
    earlier, out_ref, gathered = refs[count + 1 : -2], *refs[-2:]
    steps, rows, width = parts[0].shape
    resident, rank, _ = down_ref.shape
    pad_rows = gathered.shape[0] // count
    for j, ref in enumerate(parts):
        for t in range(steps):
            at = j * pad_rows + t * rows
            gathered[at : at + rows, :] = ref[t].astype(F32)
        at = j * pad_rows + steps * rows
        gathered[at : (j + 1) * pad_rows, :] = jnp.zeros((pad_rows - steps * rows, width), F32)
    result = dot(
        gathered[...].astype(BF16), down_ref[...].reshape(resident * rank, width), ((1,), (1,))
    )
    for ref in earlier:
        out_ref[: ref.shape[0], :] = ref[...]
    out_ref[out_ref.shape[0] - result.shape[0] :, :] = result


def own_rank_kernel(own_ref, down_ref, out_ref, kept_ref, gathered):
    rank_kernel(1, own_ref, down_ref, out_ref, gathered)
    kept_ref[...] = down_ref[...]


def copy_kernel(in_ref, _, out_ref):
    out_ref[...] = in_ref[...]


def query_kernel(parts, block, *refs):
    rank_refs = refs[:parts]
    up_ref, base_ref, cos_ref, sin_ref = refs[parts : parts + 4]
    out_ref, ids_ref = refs[-2:]
    resident, rank, _ = up_ref.shape
    steps, rows, width = out_ref.shape
    pad_rows = ids_ref.shape[0]
    ids_ref[...] = jnp.zeros_like(ids_ref)
    for t in range(steps):
        ids_ref[t * rows : (t + 1) * rows, :] = base_ref[t, :, width:].astype(F32)
    ids = ids_ref[:, LANES // 2 : LANES // 2 + 1].astype(jnp.int32)
    ranks = functools.reduce(
        jnp.add, [ref[block * pad_rows : (block + 1) * pad_rows, :] for ref in rank_refs]
    )
    lane = lax.broadcasted_iota(jnp.int32, ranks.shape, 1)
    owner = lax.axis_index("adapter") * resident + lane // rank
    chosen = jnp.where(owner == ids, ranks, 0.0).astype(BF16)
    correction = dot(chosen, up_ref[...].reshape(resident * rank, width), ((1,), (0,)))
    for t in range(steps):
        cos_part, sin_part = cos_ref[t], sin_ref[t]
        for h in range(width // HEAD_SIZE):
            at = slice(h * HEAD_SIZE, (h + 1) * HEAD_SIZE)
            piece = base_ref[t, :, at].astype(F32) + correction[t * rows : (t + 1) * rows, at]
            turned = piece * cos_part + pltpu.roll(piece, HEAD_SIZE // 2, 1) * sin_part
            out_ref[t, :, at] = turned.astype(BF16)


def pick_kernel(adapters, resident, *refs):
    queries = refs[:adapters]
    base_ref, _, out_ref, meta_ref = refs[adapters:]
    meta_ref[...] = base_ref[0, :, out_ref.shape[2] :].astype(F32).astype(jnp.int32)
    owner = meta_ref[:, LANES // 2 : LANES // 2 + 1] // resident
    x = lax.axis_index("adapter")
    for t in range(out_ref.shape[0]):
        picked = queries[0][t].astype(F32)
        for j in range(1, adapters):
            picked = jnp.where(owner == peer(x, j, adapters), queries[j][t].astype(F32), picked)
        out_ref[t] = picked.astype(BF16)


def load_queries(query_ref, rows_ref):
    steps, rows, _ = query_ref.shape
    rows_ref[...] = jnp.zeros_like(rows_ref)
    for t in range(steps):
        rows_ref[t * rows : (t + 1) * rows, :] = query_ref[t].astype(F32)


def group_queries(rows_ref, first, group):
    pieces = [
        rows_ref[:, first + g * HEAD_SIZE : first + (g + 1) * HEAD_SIZE] for g in range(group)
    ]
    return jnp.concatenate(pieces, axis=0).astype(BF16)


def attend(query, key, value, scale, extra=None):
    scores = dot(query, key, ((1,), (1,)))
    if extra is not None:
        more_key, more_value, bias = extra
        scores = jnp.concatenate([scores, dot(query, more_key, ((1,), (1,))) + bias], axis=1)
        value = jnp.concatenate([value, more_value], axis=0)
    peaks = jnp.max(scores, axis=1, keepdims=True)
    weight = jnp.exp2((scores - peaks) * scale).astype(BF16)
    ones = jnp.ones((value.shape[0], LANES), BF16)
    summed = dot(weight, jnp.concatenate([value, ones], axis=1), ((1,), (0,)))
    total = summed[:, HEAD_SIZE:]
    return summed[:, :HEAD_SIZE] / total, peaks * scale + jnp.log2(total)


def split_stat(stat, heads):
    first = stat.astype(BF16).astype(F32)
    second = (stat - first).astype(BF16).astype(F32)
    third = stat - first - second
    lane = lax.broadcasted_iota(jnp.int32, stat.shape, 1)
    out = jnp.where(lane < heads, first, 0.0)
    out = jnp.where((lane >= heads) & (lane < 2 * heads), pltpu.roll(second, heads, 1), out)
    out = jnp.where(
        (lane >= 2 * heads) & (lane < 3 * heads), pltpu.roll(third, 2 * heads, 1), out
    )
    return out


def far_kernel(scale, query_ref, kv_ref, *refs):
    out_ref, rows_ref, kept, stats = refs[-4:]
    steps, rows, width = query_ref.shape
    heads = width // HEAD_SIZE
    kv_heads = kv_ref.shape[2] // HEAD_SIZE
    group = heads // kv_heads
    cut = rows_ref.shape[0]
    load_queries(query_ref, rows_ref)
    lane = lax.broadcasted_iota(jnp.int32, (cut, LANES), 1)
    for kv in range(kv_heads):
        at = pl.ds(kv * HEAD_SIZE, HEAD_SIZE)
        queries = group_queries(rows_ref, kv * group * HEAD_SIZE, group)
        result, level = attend(queries, kv_ref[0, :, at], kv_ref[1, :, at], scale)
        for g in range(group):
            head = kv * group + g
            kept[:, head * HEAD_SIZE : (head + 1) * HEAD_SIZE] = result[g * cut : (g + 1) * cut]
            piece = level[g * cut : (g + 1) * cut]
            stats[...] = jnp.where(lane == head, piece, stats[...] if head else 0.0)
    packed = split_stat(stats[...], heads)
    for t in range(steps):
        at = t * rows
        out_ref[t, :, :width] = kept[at : at + rows, :].astype(BF16)
        out_ref[t, :, width:] = packed[at : at + rows, :].astype(BF16)


def near_kernel(scale, query_ref, kv_ref, suffix_ref, fresh_ref, meta_ref, *refs):
    own_ref, level_ref, rows_ref, kept, stats, fresh_rows, length_rows = refs
    load_queries(query_ref, rows_ref)
    steps, rows, width = query_ref.shape
    heads = width // HEAD_SIZE
    kv_heads = kv_ref.shape[2] // HEAD_SIZE
    group = heads // kv_heads
    cut = rows_ref.shape[0]
    fresh_rows[...] = jnp.zeros_like(fresh_rows)
    length_rows[...] = jnp.zeros_like(length_rows)
    for t in range(steps):
        length_rows[t * rows : (t + 1) * rows, :] = meta_ref[...]
        for part in range(2):
            fresh_rows[part, t * rows : (t + 1) * rows, :] = fresh_ref[part, t].astype(F32)
    slots = suffix_ref.shape[2]
    suffix_count = rows * slots
    shape = (cut, suffix_count + fresh_rows.shape[1])
    token = lax.broadcasted_iota(jnp.int32, shape, 0)
    column = lax.broadcasted_iota(jnp.int32, shape, 1)
    token_row, token_step = token % rows, token // rows
    fresh_at = column - suffix_count
    in_suffix = (column < suffix_count) & (column // slots == token_row)
    in_suffix &= column % slots < length_rows[:, 0:1]
    in_fresh = (column >= suffix_count) & (fresh_at % rows == token_row)
    in_fresh &= fresh_at // rows <= token_step
    bias = jnp.where(in_suffix | in_fresh, 0.0, MASKED)
    bias = jnp.concatenate([bias] * group, axis=0)
    lane = lax.broadcasted_iota(jnp.int32, (cut, LANES), 1)
    for kv in range(kv_heads):
        at = pl.ds(kv * HEAD_SIZE, HEAD_SIZE)
        more = [
            jnp.concatenate(
                [suffix_ref[part, r, :, at] for r in range(rows)]
                + [fresh_rows[part, :, at].astype(BF16)],
                axis=0,
            )
            for part in range(2)
        ]
        result, level = attend(
            group_queries(rows_ref, kv * group * HEAD_SIZE, group),
            kv_ref[0, :, at],
            kv_ref[1, :, at],
            scale,
            (more[0], more[1], bias),
        )
        for g in range(group):
            head = kv * group + g
            kept[:, head * HEAD_SIZE : (head + 1) * HEAD_SIZE] = result[g * cut : (g + 1) * cut]
            piece = level[g * cut : (g + 1) * cut]
            stats[...] = jnp.where(lane == head, piece, stats[...] if head else 0.0)
    for t in range(steps):
        own_ref[t] = kept[t * rows : (t + 1) * rows, :]
        level_ref[t] = stats[t * rows : (t + 1) * rows, :]


def message_levels(packed, heads):
    count = packed.shape[1]
    return (
        packed + pltpu.roll(packed, count - heads, 1) + pltpu.roll(packed, count - 2 * heads, 1)
    )


def mix(own_ref, level_ref, arrived, t, store):
    width = own_ref.shape[2]
    heads = width // HEAD_SIZE
    levels = [level_ref[t]]
    for ref in arrived:
        levels.append(message_levels(ref[t, :, width:].astype(F32), heads))
    highest = functools.reduce(jnp.maximum, levels)
    shares = [jnp.exp2(level - highest) for level in levels]
    total = functools.reduce(jnp.add, shares)
    shares = [share / total for share in shares]
    for h in range(heads):
        at = slice(h * HEAD_SIZE, (h + 1) * HEAD_SIZE)
        mixed = own_ref[t, :, at] * shares[0][:, h : h + 1]
        for ref, share in zip(arrived, shares[1:]):
            mixed += ref[t, :, at].astype(F32) * share[:, h : h + 1]
        store(at, mixed)
    return highest + jnp.log2(total)


def blend_kernel(*refs):
    arrived = refs[:-4]
    own_ref, level_ref, out_ref, out_level_ref = refs[-4:]
    for t in range(own_ref.shape[0]):

        def store(at, mixed):
            out_ref[t, :, at] = mixed

        out_level_ref[t] = mix(own_ref, level_ref, arrived, t, store)


def merge_kernel(messages, adapters, *refs):
    arrived = refs[:messages]
    own_ref, level_ref = refs[messages : messages + 2]
    downs = refs[2 + messages : 2 + messages + adapters]
    meta_ref, out_hbm, rank_ref, rows_ref, ids_ref, out_ref, sem = refs[2 + messages + adapters :]
    steps, rows, _ = own_ref.shape
    resident, rank, _ = downs[0].shape
    depth = resident * rank
    x = lax.axis_index("adapter")
    rows_ref[...] = jnp.zeros_like(rows_ref)
    ids_ref[...] = jnp.zeros_like(ids_ref)
    for t in range(steps):
        ids_ref[t * rows : (t + 1) * rows, :] = meta_ref[...]

        def store(at, mixed):
            out_ref[t, :, at] = mixed.astype(BF16)
            rows_ref[t * rows : (t + 1) * rows, at] = mixed

        mix(own_ref, level_ref, arrived, t, store)
    copy = pltpu.make_async_copy(out_ref, out_hbm, sem)
    copy.start()
    factors = jnp.concatenate([down[u] for down in downs for u in range(resident)], axis=0)
    result = dot(rows_ref[...].astype(BF16), factors, ((1,), (1,)))
    lane = lax.broadcasted_iota(jnp.int32, result.shape, 1)
    owner = peer(x, lane // depth, adapters) * resident + lane % depth // rank
    rank_ref[...] = jnp.where(owner == ids_ref[:, LANES // 2 : LANES // 2 + 1], result, 0.0)
    copy.wait()


def up_kernel(parts, adapters, *refs):
    ranks = refs[:parts]
    ups = refs[parts : parts + adapters]
    out_ref = refs[parts + adapters]
    steps, rows, width = out_ref.shape
    resident = ups[0].shape[0]
    chosen = functools.reduce(jnp.add, [ref[...] for ref in ranks]).astype(BF16)
    factors = jnp.concatenate([up[u] for up in ups for u in range(resident)], axis=0)
    result = dot(chosen, factors, ((1,), (0,)))
    for t in range(steps):
        out_ref[t] = result[t * rows : (t + 1) * rows].astype(BF16)


def rope_parts(lengths, steps, first_position):
    half_dim = HEAD_SIZE // 2
    frequency = rope_base ** (-2.0 * jnp.arange(half_dim, dtype=F32) / HEAD_SIZE)
    lengths = lengths.astype(jnp.int32)
    position = first_position + lengths + jnp.arange(steps, dtype=jnp.int32)[:, None]
    angles = position.astype(F32)[..., None] * frequency
    cos_part, sin_part = jnp.cos(angles), jnp.sin(angles)
    return (
        jnp.concatenate([cos_part, cos_part], axis=-1),
        jnp.concatenate([-sin_part, sin_part], axis=-1),
    )


def on_device(
    hidden,
    base_query_rows,
    fresh_key_value,
    suffix_key_value,
    suffix_length,
    row_adapter_index,
    prompt_key_value,
    query_down_factors,
    query_up_factors,
    output_down_factors,
    output_up_factors,
):
    rows, steps, width = hidden.shape
    seq_count, adapters, halves = (lax.axis_size(name) for name in ("seq", "adapter", "head"))
    slots = suffix_key_value.shape[2]
    resident, rank, _ = query_down_factors.shape
    depth = resident * rank
    tokens = rows * steps
    pad_rows = -(-tokens // 16) * 16
    heads = width // HEAD_SIZE
    kv_heads = prompt_key_value.shape[2] // HEAD_SIZE
    group = heads // kv_heads
    scale = math.log2(math.e) / math.sqrt(HEAD_SIZE)
    stat_lanes = -(-3 * heads // LANES) * LANES
    hidden = hidden.transpose(1, 0, 2)
    lane = jnp.arange(LANES, dtype=jnp.int32)
    facts = jnp.where(lane < LANES // 2, suffix_length[:, None], row_adapter_index).astype(BF16)
    base = jnp.concatenate([base_query_rows.transpose(1, 0, 2), jnp.broadcast_to(facts, (steps, rows, LANES))], axis=2)
    fresh = fresh_key_value.transpose(0, 2, 1, 3)

    own_rows = jax.ShapeDtypeStruct((pad_rows, depth), F32)
    factors = jax.ShapeDtypeStruct(query_down_factors.shape, BF16)
    own_ranks, own_down = call(
        own_rank_kernel,
        (own_rows, factors),
        (hidden, query_down_factors),
        scratch=[pltpu.VMEM((pad_rows, width), F32)],
    )
    hidden_of = [fetch(hidden, "adapter", j) for j in range(1, adapters)]
    ranks = call(
        functools.partial(rank_kernel, adapters - 1),
        jax.ShapeDtypeStruct((adapters * pad_rows, depth), F32),
        (*hidden_of, own_down, own_ranks),
        scratch=[pltpu.VMEM(((adapters - 1) * pad_rows, width), F32)],
    )
    rank_parts = [ranks] + [fetch(ranks, "head", j) for j in range(1, halves)]
    own_up = call(
        copy_kernel,
        jax.ShapeDtypeStruct(query_up_factors.shape, BF16),
        (query_up_factors, ranks),
    )
    first_position = prompt_key_value.shape[1] * seq_count
    block_queries = []
    for j in reversed(range(adapters)):
        block_base = fetch(base, "adapter", j) if j else base
        block_queries.insert(
            0,
            call(
                functools.partial(query_kernel, halves, j),
                jax.ShapeDtypeStruct((steps, rows, width), BF16),
                (
                    *rank_parts,
                    own_up,
                    block_base,
                    *rope_parts(block_base[0, :, width], steps, first_position),
                    *block_queries[:1],
                ),
                scratch=[pltpu.VMEM((pad_rows, LANES), F32)],
            ),
        )
    arrived = [send(part, "adapter", j) for j, part in enumerate(block_queries) if j]
    output_down_factors, output_up_factors, token = lax.optimization_barrier(
        (output_down_factors, output_up_factors, block_queries[0][0, :, :LANES])
    )
    queries, meta = call(
        functools.partial(pick_kernel, adapters, resident),
        (
            jax.ShapeDtypeStruct((steps, rows, width), BF16),
            jax.ShapeDtypeStruct((rows, LANES), jnp.int32),
        ),
        (block_queries[0], *arrived, base, token),
        flops=1 << 36,
    )
    message = jax.ShapeDtypeStruct((steps, rows, width + stat_lanes), BF16)
    query_scratch = [
        pltpu.VMEM((pad_rows, width), F32),
        pltpu.VMEM((pad_rows, width), F32),
        pltpu.VMEM((pad_rows, LANES), F32),
    ]
    piece_of = {0: queries}
    for k in range(1, seq_count):
        piece_of[k] = fetch(piece_of[k - 1], "seq", 1) if k % 2 else fetch(queries, "seq", k)
    order = list(range(2, seq_count)) + [1]
    messages = []
    for k in order:
        messages.append(
            call(
                functools.partial(far_kernel, scale),
                message,
                (piece_of[k], prompt_key_value),
                scratch=query_scratch,
            )
        )
    fresh_slots = -(-tokens // LANES) * LANES
    part_shapes = (
        jax.ShapeDtypeStruct((steps, rows, width), F32),
        jax.ShapeDtypeStruct((steps, rows, LANES), F32),
    )
    own, level = call(
        functools.partial(near_kernel, scale),
        part_shapes,
        (queries, prompt_key_value, suffix_key_value, fresh, meta),
        scratch=query_scratch
        + [
            pltpu.VMEM((2, fresh_slots, fresh.shape[3]), F32),
            pltpu.VMEM((pad_rows, LANES), jnp.int32),
        ],
    )
    output_downs = [output_down_factors] + [
        fetch(output_down_factors, "adapter", j) for j in range(1, adapters)
    ]
    output_ups = [output_up_factors] + [
        fetch(output_up_factors, "adapter", j) for j in range(1, adapters)
    ]
    partials = [send(part, "seq", k) for part, k in zip(messages, order)]
    early, partials = partials[:-2], partials[-2:]
    if early:
        own, level = call(blend_kernel, part_shapes, (*early, own, level))
    attended, out_rank = call(
        functools.partial(merge_kernel, len(partials), adapters),
        (
            jax.ShapeDtypeStruct((steps, rows, width), BF16),
            jax.ShapeDtypeStruct((pad_rows, adapters * depth), F32),
        ),
        (*partials, own, level, *output_downs, meta),
        scratch=[
            pltpu.VMEM((pad_rows, width), F32),
            pltpu.VMEM((pad_rows, LANES), jnp.int32),
            pltpu.VMEM((steps, rows, width), BF16),
            pltpu.SemaphoreType.DMA,
        ],
        out_specs=(pl.BlockSpec(memory_space=pl.ANY), VMEM),
    )
    out_ranks = [out_rank] + [fetch(out_rank, "head", j) for j in range(1, halves)]
    adapted = call(
        functools.partial(up_kernel, halves, adapters),
        jax.ShapeDtypeStruct((steps, rows, width), BF16),
        (*out_ranks, *output_ups),
    )
    return attended.transpose(1, 0, 2), adapted.transpose(1, 0, 2)


def solution(mesh):
    rows = ("groups", "seq", "adapter")
    factors = P(("groups", "adapter"), None, "head")
    placed = (
        P(rows, None, "head"),
        P(rows, None, "head"),
        P(None, rows, None, "head"),
        P(None, rows, None, "head"),
        P(rows),
        P(rows, None),
        P(None, ("groups", "seq"), "head"),
        factors,
        factors,
        factors,
        factors,
    )
    return jax.shard_map(
        on_device,
        mesh=mesh,
        in_specs=placed,
        out_specs=(P(rows, None, "head"), P(rows, None, "head")),
        check_vma=False,
    )
```

```python
import functools
import math

import jax
import jax.numpy as jnp
from jax import lax
from jax.experimental import pallas as pl
from jax.experimental.pallas import tpu as pltpu
from jax.sharding import PartitionSpec as P

HEAD_SIZE = 128
LANES = 128
rope_base = 1000000.0
MASKED = -1e30
VMEM_BYTES = 8 << 20

VMEM = pl.BlockSpec(memory_space=pltpu.VMEM)
F32 = jnp.float32
BF16 = jnp.bfloat16


def peer(index, offset, size):
    if size & (size - 1) == 0:
        return index ^ offset
    return (index + offset) % size


def fetch(value, axis, offset):
    size = lax.axis_size(axis)
    return lax.ppermute(value, axis, [(peer(i, offset, size), i) for i in range(size)])


def send(value, axis, offset):
    size = lax.axis_size(axis)
    return lax.ppermute(value, axis, [(i, peer(i, offset, size)) for i in range(size)])


def dot(left, right, contract):
    return lax.dot_general(left, right, (contract, ((), ())), preferred_element_type=F32)


def call(kernel, out_shape, args, specs=None, scratch=(), flops=1 << 20, out_specs=None):
    return pl.pallas_call(
        kernel,
        out_shape=out_shape,
        in_specs=specs or [VMEM] * len(args),
        out_specs=out_specs or jax.tree.map(lambda unused: VMEM, out_shape),
        scratch_shapes=scratch,
        compiler_params=pltpu.CompilerParams(vmem_limit_bytes=VMEM_BYTES),
        cost_estimate=pl.CostEstimate(flops=flops, bytes_accessed=1 << 20, transcendentals=0),
    )(*args)


def rank_kernel(count, *refs):
    parts = refs[:count]
    down_ref = refs[count]
    earlier, out_ref, gathered = refs[count + 1 : -2], *refs[-2:]
    steps, rows, width = parts[0].shape
    resident, rank, _ = down_ref.shape
    pad_rows = gathered.shape[0] // count
    for j, ref in enumerate(parts):
        for t in range(steps):
            at = j * pad_rows + t * rows
            gathered[at : at + rows, :] = ref[t].astype(F32)
        at = j * pad_rows + steps * rows
        gathered[at : (j + 1) * pad_rows, :] = jnp.zeros((pad_rows - steps * rows, width), F32)
    result = dot(
        gathered[...].astype(BF16), down_ref[...].reshape(resident * rank, width), ((1,), (1,))
    )
    for ref in earlier:
        out_ref[: ref.shape[0], :] = ref[...]
    out_ref[out_ref.shape[0] - result.shape[0] :, :] = result


def first_kernel(out_ref):
    out_ref[...] = jnp.zeros_like(out_ref)


def own_rank_kernel(own_ref, down_ref, table_ref, _, out_ref, kept_ref, split_ref, gathered):
    width = table_ref.shape[1]
    rest = table_ref[...]
    for i in range(3):
        part = rest.astype(BF16)
        split_ref[:, i * width : (i + 1) * width] = part
        rest = rest - part.astype(F32)
    rank_kernel(1, own_ref, down_ref, out_ref, gathered)
    kept_ref[...] = down_ref[...]


def copy_kernel(in_ref, _, out_ref):
    out_ref[...] = in_ref[...]


def query_kernel(parts, block, *refs):
    rank_refs = refs[:parts]
    up_ref, base_ref, table_ref = refs[parts : parts + 3]
    out_ref, facts_ref, angles_ref = refs[-3:]
    resident, rank, _ = up_ref.shape
    steps, rows, width = out_ref.shape
    pad_rows = facts_ref.shape[0]
    facts_ref[...] = jnp.zeros_like(facts_ref)
    for t in range(steps):
        facts_ref[t * rows : (t + 1) * rows, :] = base_ref[t, :, width:].astype(F32)
    ids = facts_ref[:, LANES // 2 : LANES // 2 + 1].astype(jnp.int32)
    shape = (pad_rows, table_ref.shape[0])
    step = lax.broadcasted_iota(jnp.int32, shape, 0) // rows
    place = (lax.broadcasted_iota(jnp.int32, shape, 1) - step).astype(F32)
    picked = (place == facts_ref[:, 0:1]).astype(F32).astype(BF16)
    found = dot(picked, table_ref[...], ((1,), (0,)))
    angles_ref[...] = found[:, : 2 * LANES] + found[:, 2 * LANES : 4 * LANES] + found[:, 4 * LANES :]
    ranks = functools.reduce(
        jnp.add, [ref[block * pad_rows : (block + 1) * pad_rows, :] for ref in rank_refs]
    )
    lane = lax.broadcasted_iota(jnp.int32, ranks.shape, 1)
    owner = lax.axis_index("adapter") * resident + lane // rank
    chosen = jnp.where(owner == ids, ranks, 0.0).astype(BF16)
    correction = dot(chosen, up_ref[...].reshape(resident * rank, width), ((1,), (0,)))
    for t in range(steps):
        cos_part = angles_ref[t * rows : (t + 1) * rows, :LANES]
        sin_part = angles_ref[t * rows : (t + 1) * rows, LANES:]
        for h in range(width // HEAD_SIZE):
            at = slice(h * HEAD_SIZE, (h + 1) * HEAD_SIZE)
            piece = base_ref[t, :, at].astype(F32) + correction[t * rows : (t + 1) * rows, at]
            turned = piece * cos_part + pltpu.roll(piece, HEAD_SIZE // 2, 1) * sin_part
            out_ref[t, :, at] = turned.astype(BF16)


def pick_kernel(adapters, resident, *refs):
    queries = refs[:adapters]
    base_ref, _, out_ref, meta_ref = refs[adapters:]
    meta_ref[...] = base_ref[0, :, out_ref.shape[2] :].astype(F32).astype(jnp.int32)
    owner = meta_ref[:, LANES // 2 : LANES // 2 + 1] // resident
    x = lax.axis_index("adapter")
    for t in range(out_ref.shape[0]):
        picked = queries[0][t].astype(F32)
        for j in range(1, adapters):
            picked = jnp.where(owner == peer(x, j, adapters), queries[j][t].astype(F32), picked)
        out_ref[t] = picked.astype(BF16)


def load_queries(query_ref, rows_ref):
    steps, rows, _ = query_ref.shape
    rows_ref[...] = jnp.zeros_like(rows_ref)
    for t in range(steps):
        rows_ref[t * rows : (t + 1) * rows, :] = query_ref[t].astype(F32)


def group_queries(rows_ref, first, group):
    pieces = [
        rows_ref[:, first + g * HEAD_SIZE : first + (g + 1) * HEAD_SIZE] for g in range(group)
    ]
    return jnp.concatenate(pieces, axis=0).astype(BF16)


def attend(queries, keys, values, scale):
    scores = []
    for query, parts in zip(queries, keys):
        found = []
        for key, bias in parts:
            part = dot(query, key, ((1,), (1,)))
            found.append(part if bias is None else part + bias)
        scores.append(found[0] if len(found) == 1 else jnp.concatenate(found, axis=1))
    peaks = [jnp.max(score, axis=1, keepdims=True) * scale for score in scores]
    weights = [jnp.exp2(s * scale - p).astype(BF16) for s, p in zip(scores, peaks)]
    for weight, peak, parts in zip(weights, peaks, values):
        value = parts[0] if len(parts) == 1 else jnp.concatenate(parts, axis=0)
        ones = jnp.ones((value.shape[0], LANES), BF16)
        summed = dot(weight, jnp.concatenate([value, ones], axis=1), ((1,), (0,)))
        total = summed[:, HEAD_SIZE:]
        yield summed[:, :HEAD_SIZE] * (1.0 / total), peak + jnp.log2(total)


def split_stat(stat, heads):
    first = stat.astype(BF16).astype(F32)
    second = (stat - first).astype(BF16).astype(F32)
    third = stat - first - second
    lane = lax.broadcasted_iota(jnp.int32, stat.shape, 1)
    out = jnp.where(lane < heads, first, 0.0)
    out = jnp.where((lane >= heads) & (lane < 2 * heads), pltpu.roll(second, heads, 1), out)
    out = jnp.where(
        (lane >= 2 * heads) & (lane < 3 * heads), pltpu.roll(third, 2 * heads, 1), out
    )
    return out


def far_kernel(scale, query_ref, kv_ref, out_ref, rows_ref, kept, stats_ref):
    steps, rows, width = query_ref.shape
    heads = width // HEAD_SIZE
    kv_heads = kv_ref.shape[2] // HEAD_SIZE
    group = heads // kv_heads
    cut = rows_ref.shape[0]
    load_queries(query_ref, rows_ref)
    columns = [slice(kv * HEAD_SIZE, (kv + 1) * HEAD_SIZE) for kv in range(kv_heads)]
    found = attend(
        [group_queries(rows_ref, kv * group * HEAD_SIZE, group) for kv in range(kv_heads)],
        [[(kv_ref[0, :, at], None)] for at in columns],
        [[kv_ref[1, :, at]] for at in columns],
        scale,
    )
    stats_ref[...] = split_stat(collect(found, kept, cut, group), heads)
    for t in range(steps):
        at = t * rows
        out_ref[t, :, :width] = kept[at : at + rows, :].astype(BF16)
        out_ref[t, :, width:] = stats_ref[at : at + rows, :].astype(BF16)


def collect(found, kept, cut, group):
    lane = lax.broadcasted_iota(jnp.int32, (cut, LANES), 1)
    stats = jnp.zeros((cut, LANES), F32)
    for kv, (result, level) in enumerate(found):
        for g in range(group):
            head = kv * group + g
            kept[:, head * HEAD_SIZE : (head + 1) * HEAD_SIZE] = result[g * cut : (g + 1) * cut]
            stats = jnp.where(lane == head, level[g * cut : (g + 1) * cut], stats)
    return stats


def near_kernel(scale, query_ref, kv_ref, suffix_ref, fresh_ref, meta_ref, *refs):
    own_ref, level_ref, rows_ref, kept, stats, fresh_rows, length_rows = refs
    load_queries(query_ref, rows_ref)
    steps, rows, width = query_ref.shape
    heads = width // HEAD_SIZE
    kv_heads = kv_ref.shape[2] // HEAD_SIZE
    group = heads // kv_heads
    cut = rows_ref.shape[0]
    fresh_rows[...] = jnp.zeros_like(fresh_rows)
    length_rows[...] = jnp.zeros_like(length_rows)
    for t in range(steps):
        length_rows[t * rows : (t + 1) * rows, :] = meta_ref[...]
        for part in range(2):
            fresh_rows[part, t * rows : (t + 1) * rows, :] = fresh_ref[part, t].astype(F32)
    slots = suffix_ref.shape[2]
    suffix_count = rows * slots
    shape = (cut, suffix_count + fresh_rows.shape[1])
    token = lax.broadcasted_iota(jnp.int32, shape, 0)
    column = lax.broadcasted_iota(jnp.int32, shape, 1)
    token_row, token_step = token % rows, token // rows
    fresh_at = column - suffix_count
    in_suffix = (column < suffix_count) & (column // slots == token_row)
    in_suffix &= column % slots < length_rows[:, 0:1]
    in_fresh = (column >= suffix_count) & (fresh_at % rows == token_row)
    in_fresh &= fresh_at // rows <= token_step
    bias = jnp.where(in_suffix | in_fresh, 0.0, MASKED)
    bias = jnp.concatenate([bias] * group, axis=0)
    columns = [slice(kv * HEAD_SIZE, (kv + 1) * HEAD_SIZE) for kv in range(kv_heads)]

    def local(part, at):
        pieces = [suffix_ref[part, r, :, at] for r in range(rows)]
        return jnp.concatenate(pieces + [fresh_rows[part, :, at].astype(BF16)], axis=0)

    found = attend(
        [group_queries(rows_ref, kv * group * HEAD_SIZE, group) for kv in range(kv_heads)],
        [[(kv_ref[0, :, at], None), (local(0, at), bias)] for at in columns],
        [[kv_ref[1, :, at], local(1, at)] for at in columns],
        scale,
    )
    stats[...] = collect(found, kept, cut, group)
    for t in range(steps):
        own_ref[t] = kept[t * rows : (t + 1) * rows, :]
        level_ref[t] = stats[t * rows : (t + 1) * rows, :]


def message_levels(packed, heads):
    count = packed.shape[1]
    return (
        packed + pltpu.roll(packed, count - heads, 1) + pltpu.roll(packed, count - 2 * heads, 1)
    )


def mix(own_ref, level_ref, arrived, t, store):
    width = own_ref.shape[2]
    heads = width // HEAD_SIZE
    levels = [level_ref[t]]
    for ref in arrived:
        levels.append(message_levels(ref[t, :, width:].astype(F32), heads))
    highest = functools.reduce(jnp.maximum, levels)
    shares = [jnp.exp2(level - highest) for level in levels]
    total = functools.reduce(jnp.add, shares)
    shares = [share / total for share in shares]
    for h in range(heads):
        at = slice(h * HEAD_SIZE, (h + 1) * HEAD_SIZE)
        mixed = own_ref[t, :, at] * shares[0][:, h : h + 1]
        for ref, share in zip(arrived, shares[1:]):
            mixed += ref[t, :, at].astype(F32) * share[:, h : h + 1]
        store(at, mixed)
    return highest + jnp.log2(total)


def blend_kernel(*refs):
    arrived = refs[:-4]
    own_ref, level_ref, out_ref, out_level_ref = refs[-4:]
    for t in range(own_ref.shape[0]):

        def store(at, mixed):
            out_ref[t, :, at] = mixed

        out_level_ref[t] = mix(own_ref, level_ref, arrived, t, store)


def merge_kernel(messages, adapters, *refs):
    arrived = refs[:messages]
    own_ref, level_ref = refs[messages : messages + 2]
    downs = refs[2 + messages : 2 + messages + adapters]
    meta_ref, out_hbm, rank_ref, rows_ref, ids_ref, out_ref, sem = refs[2 + messages + adapters :]
    steps, rows, _ = own_ref.shape
    resident, rank, _ = downs[0].shape
    depth = resident * rank
    x = lax.axis_index("adapter")
    rows_ref[...] = jnp.zeros_like(rows_ref)
    ids_ref[...] = jnp.zeros_like(ids_ref)
    for t in range(steps):
        ids_ref[t * rows : (t + 1) * rows, :] = meta_ref[...]

        def store(at, mixed):
            out_ref[t, :, at] = mixed.astype(BF16)
            rows_ref[t * rows : (t + 1) * rows, at] = mixed

        mix(own_ref, level_ref, arrived, t, store)
    copy = pltpu.make_async_copy(out_ref, out_hbm, sem)
    copy.start()
    factors = jnp.concatenate([down[u] for down in downs for u in range(resident)], axis=0)
    result = dot(rows_ref[...].astype(BF16), factors, ((1,), (1,)))
    lane = lax.broadcasted_iota(jnp.int32, result.shape, 1)
    owner = peer(x, lane // depth, adapters) * resident + lane % depth // rank
    rank_ref[...] = jnp.where(owner == ids_ref[:, LANES // 2 : LANES // 2 + 1], result, 0.0)
    copy.wait()


def up_kernel(parts, adapters, *refs):
    ranks = refs[:parts]
    ups = refs[parts : parts + adapters]
    out_ref = refs[parts + adapters]
    steps, rows, width = out_ref.shape
    resident = ups[0].shape[0]
    chosen = functools.reduce(jnp.add, [ref[...] for ref in ranks]).astype(BF16)
    factors = jnp.concatenate([up[u] for up in ups for u in range(resident)], axis=0)
    result = dot(chosen, factors, ((1,), (0,)))
    for t in range(steps):
        out_ref[t] = result[t * rows : (t + 1) * rows].astype(BF16)


def rope_table(slots, first_position):
    half_dim = HEAD_SIZE // 2
    frequency = rope_base ** (-2.0 * jnp.arange(half_dim, dtype=F32) / HEAD_SIZE)
    position = (first_position + jnp.arange(slots, dtype=jnp.int32)).astype(F32)
    angles = position[:, None] * frequency
    cos_part, sin_part = jnp.cos(angles), jnp.sin(angles)
    return jnp.concatenate([cos_part, cos_part, -sin_part, sin_part], axis=1)


def on_device(
    hidden,
    base_query_rows,
    fresh_key_value,
    suffix_key_value,
    suffix_length,
    row_adapter_index,
    prompt_key_value,
    query_down_factors,
    query_up_factors,
    output_down_factors,
    output_up_factors,
):
    rows, steps, width = hidden.shape
    seq_count, adapters, halves = (lax.axis_size(name) for name in ("seq", "adapter", "head"))
    slots = suffix_key_value.shape[2]
    resident, rank, _ = query_down_factors.shape
    depth = resident * rank
    tokens = rows * steps
    pad_rows = -(-tokens // 16) * 16
    heads = width // HEAD_SIZE
    kv_heads = prompt_key_value.shape[2] // HEAD_SIZE
    group = heads // kv_heads
    scale = math.log2(math.e) / math.sqrt(HEAD_SIZE)
    stat_lanes = -(-3 * heads // LANES) * LANES
    hidden = hidden.transpose(1, 0, 2)
    lane = lax.broadcasted_iota(jnp.int32, (steps, rows, width + LANES), 2)
    facts = jnp.where(lane < width + LANES // 2, suffix_length[:, None], row_adapter_index)
    base = jnp.pad(base_query_rows.transpose(1, 0, 2), ((0, 0), (0, 0), (0, LANES)))
    base = jnp.where(lane < width, base, facts.astype(BF16))
    fresh = fresh_key_value.transpose(0, 2, 1, 3)

    own_rows = jax.ShapeDtypeStruct((pad_rows, depth), F32)
    factors = jax.ShapeDtypeStruct(query_down_factors.shape, BF16)
    first = call(first_kernel, jax.ShapeDtypeStruct((8, LANES), F32), (), flops=1 << 34)
    table_slots = -(-(slots + steps) // 16) * 16
    table = rope_table(table_slots, prompt_key_value.shape[1] * seq_count)
    own_ranks, own_down, table = call(
        own_rank_kernel,
        (own_rows, factors, jax.ShapeDtypeStruct((table_slots, 6 * LANES), BF16)),
        (hidden, query_down_factors, table, first),
        scratch=[pltpu.VMEM((pad_rows, width), F32)],
    )
    hidden_of = [fetch(hidden, "adapter", j) for j in range(1, adapters)]
    ranks = call(
        functools.partial(rank_kernel, adapters - 1),
        jax.ShapeDtypeStruct((adapters * pad_rows, depth), F32),
        (*hidden_of, own_down, own_ranks),
        scratch=[pltpu.VMEM(((adapters - 1) * pad_rows, width), F32)],
    )
    rank_parts = [ranks] + [fetch(ranks, "head", j) for j in range(1, halves)]
    own_up = call(
        copy_kernel,
        jax.ShapeDtypeStruct(query_up_factors.shape, BF16),
        (query_up_factors, ranks),
    )
    block_queries = []
    for j in reversed(range(adapters)):
        block_base = fetch(base, "adapter", j) if j else base
        block_queries.insert(
            0,
            call(
                functools.partial(query_kernel, halves, j),
                jax.ShapeDtypeStruct((steps, rows, width), BF16),
                (
                    *rank_parts,
                    own_up,
                    block_base,
                    table,
                    *block_queries[:1],
                ),
                scratch=[
                    pltpu.VMEM((pad_rows, LANES), F32),
                    pltpu.VMEM((pad_rows, 2 * LANES), F32),
                ],
            ),
        )
    arrived = [send(part, "adapter", j) for j, part in enumerate(block_queries) if j]
    output_down_factors, output_up_factors, token = lax.optimization_barrier(
        (output_down_factors, output_up_factors, block_queries[0][0, :, :LANES])
    )
    queries, meta = call(
        functools.partial(pick_kernel, adapters, resident),
        (
            jax.ShapeDtypeStruct((steps, rows, width), BF16),
            jax.ShapeDtypeStruct((rows, LANES), jnp.int32),
        ),
        (block_queries[0], *arrived, base, token),
        flops=1 << 36,
    )
    message = jax.ShapeDtypeStruct((steps, rows, width + stat_lanes), BF16)
    query_scratch = [
        pltpu.VMEM((pad_rows, width), F32),
        pltpu.VMEM((pad_rows, width), F32),
        pltpu.VMEM((pad_rows, LANES), F32),
    ]
    piece_of = {0: queries}
    for k in range(1, seq_count):
        piece_of[k] = fetch(piece_of[k - 1], "seq", 1) if k % 2 else fetch(queries, "seq", k)
    order = list(range(2, seq_count)) + [1]
    messages = []
    for k in order:
        messages.append(
            call(
                functools.partial(far_kernel, scale),
                message,
                (piece_of[k], prompt_key_value),
                scratch=query_scratch,
            )
        )
    fresh_slots = -(-tokens // LANES) * LANES
    part_shapes = (
        jax.ShapeDtypeStruct((steps, rows, width), F32),
        jax.ShapeDtypeStruct((steps, rows, LANES), F32),
    )
    own, level = call(
        functools.partial(near_kernel, scale),
        part_shapes,
        (queries, prompt_key_value, suffix_key_value, fresh, meta),
        scratch=query_scratch
        + [
            pltpu.VMEM((2, fresh_slots, fresh.shape[3]), F32),
            pltpu.VMEM((pad_rows, LANES), jnp.int32),
        ],
    )
    output_downs = [output_down_factors] + [
        fetch(output_down_factors, "adapter", j) for j in range(1, adapters)
    ]
    output_ups = [output_up_factors] + [
        fetch(output_up_factors, "adapter", j) for j in range(1, adapters)
    ]
    partials = [send(part, "seq", k) for part, k in zip(messages, order)]
    last = max(seq_count - 3, 0)
    early, partials = partials[:last] + partials[last + 1 :], partials[last : last + 1]
    if early:
        own, level = call(blend_kernel, part_shapes, (*early, own, level))
    attended, out_rank = call(
        functools.partial(merge_kernel, len(partials), adapters),
        (
            jax.ShapeDtypeStruct((steps, rows, width), BF16),
            jax.ShapeDtypeStruct((pad_rows, adapters * depth), F32),
        ),
        (*partials, own, level, *output_downs, meta),
        scratch=[
            pltpu.VMEM((pad_rows, width), F32),
            pltpu.VMEM((pad_rows, LANES), jnp.int32),
            pltpu.VMEM((steps, rows, width), BF16),
            pltpu.SemaphoreType.DMA,
        ],
        out_specs=(pl.BlockSpec(memory_space=pl.ANY), VMEM),
    )
    out_ranks = [out_rank] + [fetch(out_rank, "head", j) for j in range(1, halves)]
    adapted = call(
        functools.partial(up_kernel, halves, adapters),
        jax.ShapeDtypeStruct((steps, rows, width), BF16),
        (*out_ranks, *output_ups),
    )
    return attended.transpose(1, 0, 2), adapted.transpose(1, 0, 2)


def solution(mesh):
    rows = ("groups", "seq", "adapter")
    factors = P(("groups", "adapter"), None, "head")
    placed = (
        P(rows, None, "head"),
        P(rows, None, "head"),
        P(None, rows, None, "head"),
        P(None, rows, None, "head"),
        P(rows),
        P(rows, None),
        P(None, ("groups", "seq"), "head"),
        factors,
        factors,
        factors,
        factors,
    )
    return jax.shard_map(
        on_device,
        mesh=mesh,
        in_specs=placed,
        out_specs=(P(rows, None, "head"), P(rows, None, "head")),
        check_vma=False,
    )
```

```python
import functools
import math

import jax
import jax.numpy as jnp
from jax import lax
from jax.experimental import pallas as pl
from jax.experimental.pallas import tpu as pltpu
from jax.sharding import PartitionSpec as P

HEAD_SIZE = 128
LANES = 128
rope_base = 1000000.0
MASKED = -1e30
VMEM_BYTES = 8 << 20

VMEM = pl.BlockSpec(memory_space=pltpu.VMEM)
F32 = jnp.float32
BF16 = jnp.bfloat16


def peer(index, offset, size):
    if size & (size - 1) == 0:
        return index ^ offset
    return (index + offset) % size


def fetch(value, axis, offset):
    size = lax.axis_size(axis)
    return lax.ppermute(value, axis, [(peer(i, offset, size), i) for i in range(size)])


def send(value, axis, offset):
    size = lax.axis_size(axis)
    return lax.ppermute(value, axis, [(i, peer(i, offset, size)) for i in range(size)])


def padded(tokens):
    return -(-tokens // 16) * 16


def dot(left, right, contract):
    return lax.dot_general(left, right, (contract, ((), ())), preferred_element_type=F32)


def call(kernel, out_shape, args, specs=None, scratch=(), flops=1 << 20, out_specs=None):
    return pl.pallas_call(
        kernel,
        out_shape=out_shape,
        in_specs=specs or [VMEM] * len(args),
        out_specs=out_specs or jax.tree.map(lambda unused: VMEM, out_shape),
        scratch_shapes=scratch,
        compiler_params=pltpu.CompilerParams(vmem_limit_bytes=VMEM_BYTES),
        cost_estimate=pl.CostEstimate(flops=flops, bytes_accessed=1 << 20, transcendentals=0),
    )(*args)


def rank_kernel(count, *refs):
    parts = refs[:count]
    down_ref = refs[count]
    earlier, out_ref, gathered = refs[count + 1 : -2], *refs[-2:]
    steps, rows, width = parts[0].shape
    resident, rank, _ = down_ref.shape
    pad_rows = gathered.shape[0] // count
    for j, ref in enumerate(parts):
        for t in range(steps):
            at = j * pad_rows + t * rows
            gathered[at : at + rows, :] = ref[t].astype(F32)
        at = j * pad_rows + steps * rows
        gathered[at : (j + 1) * pad_rows, :] = jnp.zeros((pad_rows - steps * rows, width), F32)
    result = dot(
        gathered[...].astype(BF16), down_ref[...].reshape(resident * rank, width), ((1,), (1,))
    )
    for ref in earlier:
        out_ref[: ref.shape[0], :] = ref[...]
    out_ref[out_ref.shape[0] - result.shape[0] :, :] = result


def first_kernel(out_ref):
    out_ref[...] = jnp.zeros_like(out_ref)


def own_rank_kernel(own_ref, down_ref, table_ref, _, out_ref, kept_ref, split_ref, gathered):
    width = table_ref.shape[1]
    rest = table_ref[...]
    for i in range(3):
        part = rest.astype(BF16)
        split_ref[:, i * width : (i + 1) * width] = part
        rest = rest - part.astype(F32)
    rank_kernel(1, own_ref, down_ref, out_ref, gathered)
    kept_ref[...] = down_ref[...]


def copy_kernel(in_ref, _, out_ref):
    out_ref[...] = in_ref[...]


def total_ranks(rank_refs, block, pad_rows):
    parts = [ref[block * pad_rows : (block + 1) * pad_rows, :] for ref in rank_refs]
    return functools.reduce(jnp.add, parts).astype(BF16)


def correction_kernel(parts, block, *refs):
    up_ref = refs[parts]
    out_ref = refs[-1]
    resident, rank, _ = up_ref.shape
    _, steps, rows, _ = out_ref.shape
    ranks = total_ranks(refs[:parts], block, padded(steps * rows))
    for u in range(resident):
        result = dot(ranks[:, u * rank : (u + 1) * rank], up_ref[u], ((1,), (0,)))
        for t in range(steps):
            out_ref[u, t] = result[t * rows : (t + 1) * rows].astype(BF16)


def prepare_kernel(parts, *refs):
    rank_refs = refs[:parts]
    up_ref, base_ref, facts_ref, table_ref = refs[parts : parts + 4]
    sum_ref, angles_ref, token_ref, column_ref = refs[-4:]
    resident, rank, _ = up_ref.shape
    steps, rows, width = base_ref.shape
    pad_rows = column_ref.shape[0]
    column_ref[...] = jnp.zeros_like(column_ref)
    for t in range(steps):
        column_ref[t * rows : (t + 1) * rows, :] = facts_ref[...]
    ids = column_ref[:, LANES // 2 : LANES // 2 + 1]
    shape = (pad_rows, table_ref.shape[0])
    step = lax.broadcasted_iota(jnp.int32, shape, 0) // rows
    place = lax.broadcasted_iota(jnp.int32, shape, 1) - step
    picked = (place == column_ref[:, 0:1]).astype(F32).astype(BF16)
    found = dot(picked, table_ref[...], ((1,), (0,)))
    angles_ref[...] = found[:, : 2 * LANES] + found[:, 2 * LANES : 4 * LANES] + found[:, 4 * LANES :]
    ranks = total_ranks(rank_refs, 0, pad_rows)
    lane = lax.broadcasted_iota(jnp.int32, ranks.shape, 1)
    owner = lax.axis_index("adapter") * resident + lane // rank
    chosen = jnp.where(owner == ids, ranks.astype(F32), 0.0).astype(BF16)
    correction = dot(chosen, up_ref[...].reshape(resident * rank, width), ((1,), (0,)))
    for t in range(steps):
        sum_ref[t] = base_ref[t].astype(F32) + correction[t * rows : (t + 1) * rows]
    token_ref[...] = jnp.zeros_like(token_ref)


def rotate_kernel(others, *refs):
    corrections = refs[:others]
    sum_ref, angles_ref, facts_ref, _, out_ref = refs[others:]
    steps, rows, width = sum_ref.shape
    x = lax.axis_index("adapter")
    ids = facts_ref[:, LANES // 2 : LANES // 2 + 1]
    for t in range(steps):
        cos_part = angles_ref[t * rows : (t + 1) * rows, :LANES]
        sin_part = angles_ref[t * rows : (t + 1) * rows, LANES:]
        for h in range(width // HEAD_SIZE):
            at = slice(h * HEAD_SIZE, (h + 1) * HEAD_SIZE)
            piece = sum_ref[t, :, at]
            for j, ref in enumerate(corrections):
                resident = ref.shape[0]
                for u in range(resident):
                    owner = peer(x, j + 1, others + 1) * resident + u
                    piece += jnp.where(ids == owner, ref[u, t, :, at].astype(F32), 0.0)
            turned = piece * cos_part + pltpu.roll(piece, HEAD_SIZE // 2, 1) * sin_part
            out_ref[t, :, at] = turned.astype(BF16)


def load_queries(query_ref, rows_ref):
    steps, rows, _ = query_ref.shape
    rows_ref[...] = jnp.zeros_like(rows_ref)
    for t in range(steps):
        rows_ref[t * rows : (t + 1) * rows, :] = query_ref[t].astype(F32)


def group_queries(rows_ref, first, group):
    pieces = [
        rows_ref[:, first + g * HEAD_SIZE : first + (g + 1) * HEAD_SIZE] for g in range(group)
    ]
    return jnp.concatenate(pieces, axis=0).astype(BF16)


def attend(queries, keys, values, scale):
    scores = []
    for query, parts in zip(queries, keys):
        found = []
        for key, bias in parts:
            part = dot(query, key, ((1,), (1,)))
            found.append(part if bias is None else part + bias)
        scores.append(found[0] if len(found) == 1 else jnp.concatenate(found, axis=1))
    peaks = [jnp.max(score, axis=1, keepdims=True) * scale for score in scores]
    weights = [jnp.exp2(s * scale - p).astype(BF16) for s, p in zip(scores, peaks)]
    for weight, peak, parts in zip(weights, peaks, values):
        value = parts[0] if len(parts) == 1 else jnp.concatenate(parts, axis=0)
        ones = jnp.ones((value.shape[0], LANES), BF16)
        summed = dot(weight, jnp.concatenate([value, ones], axis=1), ((1,), (0,)))
        total = summed[:, HEAD_SIZE:]
        yield summed[:, :HEAD_SIZE] * (1.0 / total), peak + jnp.log2(total)


def split_stat(stat, heads):
    first = stat.astype(BF16).astype(F32)
    second = (stat - first).astype(BF16).astype(F32)
    third = stat - first - second
    lane = lax.broadcasted_iota(jnp.int32, stat.shape, 1)
    out = jnp.where(lane < heads, first, 0.0)
    out = jnp.where((lane >= heads) & (lane < 2 * heads), pltpu.roll(second, heads, 1), out)
    out = jnp.where(
        (lane >= 2 * heads) & (lane < 3 * heads), pltpu.roll(third, 2 * heads, 1), out
    )
    return out


def far_kernel(scale, query_ref, kv_ref, out_ref, rows_ref, kept, stats_ref):
    steps, rows, width = query_ref.shape
    heads = width // HEAD_SIZE
    kv_heads = kv_ref.shape[2] // HEAD_SIZE
    group = heads // kv_heads
    cut = rows_ref.shape[0]
    load_queries(query_ref, rows_ref)
    columns = [slice(kv * HEAD_SIZE, (kv + 1) * HEAD_SIZE) for kv in range(kv_heads)]
    found = attend(
        [group_queries(rows_ref, kv * group * HEAD_SIZE, group) for kv in range(kv_heads)],
        [[(kv_ref[0, :, at], None)] for at in columns],
        [[kv_ref[1, :, at]] for at in columns],
        scale,
    )
    stats_ref[...] = split_stat(collect(found, kept, cut, group), heads)
    for t in range(steps):
        at = t * rows
        out_ref[t, :, :width] = kept[at : at + rows, :].astype(BF16)
        out_ref[t, :, width:] = stats_ref[at : at + rows, :].astype(BF16)


def collect(found, kept, cut, group):
    lane = lax.broadcasted_iota(jnp.int32, (cut, LANES), 1)
    stats = jnp.zeros((cut, LANES), F32)
    for kv, (result, level) in enumerate(found):
        for g in range(group):
            head = kv * group + g
            kept[:, head * HEAD_SIZE : (head + 1) * HEAD_SIZE] = result[g * cut : (g + 1) * cut]
            stats = jnp.where(lane == head, level[g * cut : (g + 1) * cut], stats)
    return stats


def near_kernel(scale, query_ref, kv_ref, suffix_ref, fresh_ref, meta_ref, *refs):
    own_ref, level_ref, rows_ref, kept, stats, fresh_rows, length_rows = refs
    load_queries(query_ref, rows_ref)
    steps, rows, width = query_ref.shape
    heads = width // HEAD_SIZE
    kv_heads = kv_ref.shape[2] // HEAD_SIZE
    group = heads // kv_heads
    cut = rows_ref.shape[0]
    fresh_rows[...] = jnp.zeros_like(fresh_rows)
    length_rows[...] = jnp.zeros_like(length_rows)
    for t in range(steps):
        length_rows[t * rows : (t + 1) * rows, :] = meta_ref[...]
        for part in range(2):
            fresh_rows[part, t * rows : (t + 1) * rows, :] = fresh_ref[part, t].astype(F32)
    slots = suffix_ref.shape[2]
    suffix_count = rows * slots
    shape = (cut, suffix_count + fresh_rows.shape[1])
    token = lax.broadcasted_iota(jnp.int32, shape, 0)
    column = lax.broadcasted_iota(jnp.int32, shape, 1)
    token_row, token_step = token % rows, token // rows
    fresh_at = column - suffix_count
    in_suffix = (column < suffix_count) & (column // slots == token_row)
    in_suffix &= column % slots < length_rows[:, 0:1]
    in_fresh = (column >= suffix_count) & (fresh_at % rows == token_row)
    in_fresh &= fresh_at // rows <= token_step
    bias = jnp.where(in_suffix | in_fresh, 0.0, MASKED)
    bias = jnp.concatenate([bias] * group, axis=0)
    columns = [slice(kv * HEAD_SIZE, (kv + 1) * HEAD_SIZE) for kv in range(kv_heads)]

    def local(part, at):
        pieces = [suffix_ref[part, r, :, at] for r in range(rows)]
        return jnp.concatenate(pieces + [fresh_rows[part, :, at].astype(BF16)], axis=0)

    found = attend(
        [group_queries(rows_ref, kv * group * HEAD_SIZE, group) for kv in range(kv_heads)],
        [[(kv_ref[0, :, at], None), (local(0, at), bias)] for at in columns],
        [[kv_ref[1, :, at], local(1, at)] for at in columns],
        scale,
    )
    stats[...] = collect(found, kept, cut, group)
    for t in range(steps):
        own_ref[t] = kept[t * rows : (t + 1) * rows, :]
        level_ref[t] = stats[t * rows : (t + 1) * rows, :]


def message_levels(packed, heads):
    count = packed.shape[1]
    return (
        packed + pltpu.roll(packed, count - heads, 1) + pltpu.roll(packed, count - 2 * heads, 1)
    )


def mix(own_ref, level_ref, arrived, store, finish=None):
    steps, _, width = own_ref.shape
    heads = width // HEAD_SIZE
    shares, levels = [], []
    for t in range(steps):
        parts = [level_ref[t]]
        for ref in arrived:
            parts.append(message_levels(ref[t, :, width:].astype(F32), heads))
        highest = functools.reduce(jnp.maximum, parts)
        weights = [jnp.exp2(part - highest) for part in parts]
        total = functools.reduce(jnp.add, weights)
        inverse = 1.0 / total
        shares.append([weight * inverse for weight in weights])
        levels.append(highest + jnp.log2(total))
    quarter = heads // 4 if heads % 4 == 0 else heads
    for h in range(heads):
        at = slice(h * HEAD_SIZE, (h + 1) * HEAD_SIZE)
        for t in range(steps):
            mixed = own_ref[t, :, at] * shares[t][0][:, h : h + 1]
            for ref, share in zip(arrived, shares[t][1:]):
                mixed += ref[t, :, at].astype(F32) * share[:, h : h + 1]
            store(t, at, mixed)
        if finish and (h + 1) % quarter == 0:
            finish(slice((h + 1 - quarter) * HEAD_SIZE, (h + 1) * HEAD_SIZE))
    return levels


def blend_kernel(*refs):
    arrived = refs[:-4]
    own_ref, level_ref, out_ref, out_level_ref = refs[-4:]

    def store(t, at, mixed):
        out_ref[t, :, at] = mixed

    for t, level in enumerate(mix(own_ref, level_ref, arrived, store)):
        out_level_ref[t] = level


def merge_kernel(messages, adapters, *refs):
    arrived = refs[:messages]
    own_ref, level_ref = refs[messages : messages + 2]
    downs = refs[2 + messages : 2 + messages + adapters]
    meta_ref, out_ref, rank_ref, rows_ref, ids_ref = refs[2 + messages + adapters :]
    steps, rows, _ = own_ref.shape
    resident, rank, _ = downs[0].shape
    depth = resident * rank
    x = lax.axis_index("adapter")
    rows_ref[...] = jnp.zeros_like(rows_ref)
    ids_ref[...] = jnp.zeros_like(ids_ref)
    for t in range(steps):
        ids_ref[t * rows : (t + 1) * rows, :] = meta_ref[...]
    products = []

    def store(t, at, mixed):
        out_ref[t, :, at] = mixed.astype(BF16)
        rows_ref[t * rows : (t + 1) * rows, at] = mixed

    def finish(at):
        factors = [down[u, :, at] for down in downs for u in range(resident)]
        products.append(
            dot(rows_ref[:, at].astype(BF16), jnp.concatenate(factors, axis=0), ((1,), (1,)))
        )

    mix(own_ref, level_ref, arrived, store, finish)
    result = functools.reduce(jnp.add, products)
    lane = lax.broadcasted_iota(jnp.int32, result.shape, 1)
    owner = peer(x, lane // depth, adapters) * resident + lane % depth // rank
    rank_ref[...] = jnp.where(owner == ids_ref[:, LANES // 2 : LANES // 2 + 1], result, 0.0)


def up_kernel(parts, adapters, *refs):
    ranks = refs[:parts]
    ups = refs[parts : parts + adapters]
    attended_ref, attended_hbm, out_hbm, out_ref, sems = refs[parts + adapters :]
    copies = [pltpu.make_async_copy(attended_ref, attended_hbm, sems.at[4])]
    copies[0].start()
    steps, rows, width = out_ref.shape
    resident = ups[0].shape[0]
    chosen = functools.reduce(jnp.add, [ref[...] for ref in ranks]).astype(BF16)
    quarter = width // 4
    for i in range(4):
        at = slice(i * quarter, (i + 1) * quarter)
        factors = jnp.concatenate([up[u, :, at] for up in ups for u in range(resident)], axis=0)
        result = dot(chosen, factors, ((1,), (0,)))
        for t in range(steps):
            out_ref[t, :, at] = result[t * rows : (t + 1) * rows].astype(BF16)
        copy = pltpu.make_async_copy(out_ref.at[:, :, at], out_hbm.at[:, :, at], sems.at[i])
        copy.start()
        copies.append(copy)
    for copy in copies:
        copy.wait()


def rope_table(slots, first_position):
    half_dim = HEAD_SIZE // 2
    frequency = rope_base ** (-2.0 * jnp.arange(half_dim, dtype=F32) / HEAD_SIZE)
    position = (first_position + jnp.arange(slots, dtype=jnp.int32)).astype(F32)
    angles = position[:, None] * frequency
    cos_part, sin_part = jnp.cos(angles), jnp.sin(angles)
    return jnp.concatenate([cos_part, cos_part, -sin_part, sin_part], axis=1)


def on_device(
    hidden,
    base_query_rows,
    fresh_key_value,
    suffix_key_value,
    suffix_length,
    row_adapter_index,
    prompt_key_value,
    query_down_factors,
    query_up_factors,
    output_down_factors,
    output_up_factors,
):
    rows, steps, width = hidden.shape
    seq_count, adapters, halves = (lax.axis_size(name) for name in ("seq", "adapter", "head"))
    slots = suffix_key_value.shape[2]
    resident, rank, _ = query_down_factors.shape
    depth = resident * rank
    tokens = rows * steps
    pad_rows = padded(tokens)
    heads = width // HEAD_SIZE
    kv_heads = prompt_key_value.shape[2] // HEAD_SIZE
    group = heads // kv_heads
    scale = math.log2(math.e) / math.sqrt(HEAD_SIZE)
    stat_lanes = -(-3 * heads // LANES) * LANES
    hidden = hidden.transpose(1, 0, 2)
    base = base_query_rows.transpose(1, 0, 2)
    lane = jnp.arange(LANES, dtype=jnp.int32)
    facts = jnp.where(lane < LANES // 2, suffix_length[:, None], row_adapter_index)
    fresh = fresh_key_value.transpose(0, 2, 1, 3)

    own_rows = jax.ShapeDtypeStruct((pad_rows, depth), F32)
    factors = jax.ShapeDtypeStruct(query_down_factors.shape, BF16)
    first = call(first_kernel, jax.ShapeDtypeStruct((8, LANES), F32), (), flops=1 << 34)
    table_slots = -(-(slots + steps) // 16) * 16
    table = rope_table(table_slots, prompt_key_value.shape[1] * seq_count)
    own_ranks, own_down, table = call(
        own_rank_kernel,
        (own_rows, factors, jax.ShapeDtypeStruct((table_slots, 6 * LANES), BF16)),
        (hidden, query_down_factors, table, first),
        scratch=[pltpu.VMEM((pad_rows, width), F32)],
    )
    hidden_of = [fetch(hidden, "adapter", j) for j in range(1, adapters)]
    ranks = call(
        functools.partial(rank_kernel, adapters - 1),
        jax.ShapeDtypeStruct((adapters * pad_rows, depth), F32),
        (*hidden_of, own_down, own_ranks),
        scratch=[pltpu.VMEM(((adapters - 1) * pad_rows, width), F32)],
    )
    rank_parts = [ranks] + [fetch(ranks, "head", j) for j in range(1, halves)]
    own_up = call(
        copy_kernel,
        jax.ShapeDtypeStruct(query_up_factors.shape, BF16),
        (query_up_factors, ranks),
    )
    corrections = [
        call(
            functools.partial(correction_kernel, halves, j),
            jax.ShapeDtypeStruct((resident, steps, rows, width), BF16),
            (*rank_parts, own_up),
        )
        for j in range(1, adapters)
    ]
    arrived = [send(part, "adapter", j + 1) for j, part in enumerate(corrections)]
    query_sum, angles, token = call(
        functools.partial(prepare_kernel, halves),
        (
            jax.ShapeDtypeStruct((steps, rows, width), F32),
            jax.ShapeDtypeStruct((pad_rows, 2 * LANES), F32),
            jax.ShapeDtypeStruct((8, LANES), F32),
        ),
        (*rank_parts, own_up, base, facts, table, *corrections),
        scratch=[pltpu.VMEM((pad_rows, LANES), jnp.int32)],
    )
    output_down_factors, output_up_factors, token = lax.optimization_barrier(
        (output_down_factors, output_up_factors, token)
    )
    queries = call(
        functools.partial(rotate_kernel, adapters - 1),
        jax.ShapeDtypeStruct((steps, rows, width), BF16),
        (*arrived, query_sum, angles, facts, token),
        flops=1 << 36,
    )
    message = jax.ShapeDtypeStruct((steps, rows, width + stat_lanes), BF16)
    query_scratch = [
        pltpu.VMEM((pad_rows, width), F32),
        pltpu.VMEM((pad_rows, width), F32),
        pltpu.VMEM((pad_rows, LANES), F32),
    ]
    piece_of = {0: queries}
    for k in range(1, seq_count):
        piece_of[k] = fetch(piece_of[k - 1], "seq", 1) if k % 2 else fetch(queries, "seq", k)
    order = list(range(2, seq_count)) + [1]
    messages = []
    for k in order:
        messages.append(
            call(
                functools.partial(far_kernel, scale),
                message,
                (piece_of[k], prompt_key_value),
                scratch=query_scratch,
            )
        )
    fresh_slots = -(-tokens // LANES) * LANES
    part_shapes = (
        jax.ShapeDtypeStruct((steps, rows, width), F32),
        jax.ShapeDtypeStruct((steps, rows, LANES), F32),
    )
    own, level = call(
        functools.partial(near_kernel, scale),
        part_shapes,
        (queries, prompt_key_value, suffix_key_value, fresh, facts),
        scratch=query_scratch
        + [
            pltpu.VMEM((2, fresh_slots, fresh.shape[3]), F32),
            pltpu.VMEM((pad_rows, LANES), jnp.int32),
        ],
    )
    output_downs = [output_down_factors] + [
        fetch(output_down_factors, "adapter", j) for j in range(1, adapters)
    ]
    output_ups = [output_up_factors] + [
        fetch(output_up_factors, "adapter", j) for j in range(1, adapters)
    ]
    partials = [send(part, "seq", k) for part, k in zip(messages, order)]
    last = max(seq_count - 3, 0)
    early, partials = partials[:last] + partials[last + 1 :], partials[last : last + 1]
    if early:
        own, level = call(blend_kernel, part_shapes, (*early, own, level))
    attended, out_rank = call(
        functools.partial(merge_kernel, len(partials), adapters),
        (
            jax.ShapeDtypeStruct((steps, rows, width), BF16),
            jax.ShapeDtypeStruct((pad_rows, adapters * depth), F32),
        ),
        (*partials, own, level, *output_downs, facts),
        scratch=[
            pltpu.VMEM((pad_rows, width), F32),
            pltpu.VMEM((pad_rows, LANES), jnp.int32),
        ],
    )
    out_ranks = [out_rank] + [fetch(out_rank, "head", j) for j in range(1, halves)]
    attended, adapted = call(
        functools.partial(up_kernel, halves, adapters),
        (jax.ShapeDtypeStruct((steps, rows, width), BF16),) * 2,
        (*out_ranks, *output_ups, attended),
        scratch=[pltpu.VMEM((steps, rows, width), BF16), pltpu.SemaphoreType.DMA((5,))],
        out_specs=(pl.BlockSpec(memory_space=pl.ANY),) * 2,
    )
    return attended.transpose(1, 0, 2), adapted.transpose(1, 0, 2)


def solution(mesh):
    rows = ("groups", "seq", "adapter")
    factors = P(("groups", "adapter"), None, "head")
    placed = (
        P(rows, None, "head"),
        P(rows, None, "head"),
        P(None, rows, None, "head"),
        P(None, rows, None, "head"),
        P(rows),
        P(rows, None),
        P(None, ("groups", "seq"), "head"),
        factors,
        factors,
        factors,
        factors,
    )
    return jax.shard_map(
        on_device,
        mesh=mesh,
        in_specs=placed,
        out_specs=(P(rows, None, "head"), P(rows, None, "head")),
        check_vma=False,
    )
```

```python
import functools
import math

import jax
import jax.numpy as jnp
from jax import lax
from jax.experimental import pallas as pl
from jax.experimental.pallas import tpu as pltpu
from jax.sharding import PartitionSpec as P

HEAD_SIZE = 128
LANES = 128
rope_base = 1000000.0
MASKED = -1e30
VMEM_BYTES = 8 << 20

VMEM = pl.BlockSpec(memory_space=pltpu.VMEM)
F32 = jnp.float32
BF16 = jnp.bfloat16


def peer(index, offset, size):
    if size & (size - 1) == 0:
        return index ^ offset
    return (index + offset) % size


def fetch(value, axis, offset):
    size = lax.axis_size(axis)
    return lax.ppermute(value, axis, [(peer(i, offset, size), i) for i in range(size)])


def send(value, axis, offset):
    size = lax.axis_size(axis)
    return lax.ppermute(value, axis, [(i, peer(i, offset, size)) for i in range(size)])


def dot(left, right, contract):
    return lax.dot_general(left, right, (contract, ((), ())), preferred_element_type=F32)


def call(kernel, out_shape, args, specs=None, scratch=(), flops=1 << 20, out_specs=None):
    return pl.pallas_call(
        kernel,
        out_shape=out_shape,
        in_specs=specs or [VMEM] * len(args),
        out_specs=out_specs or jax.tree.map(lambda unused: VMEM, out_shape),
        scratch_shapes=scratch,
        compiler_params=pltpu.CompilerParams(vmem_limit_bytes=VMEM_BYTES),
        cost_estimate=pl.CostEstimate(flops=flops, bytes_accessed=1 << 20, transcendentals=0),
    )(*args)


def rank_kernel(count, *refs):
    parts = refs[:count]
    down_ref = refs[count]
    earlier, out_ref, gathered = refs[count + 1 : -2], *refs[-2:]
    steps, rows, width = parts[0].shape
    resident, rank, _ = down_ref.shape
    pad_rows = gathered.shape[0] // count
    for j, ref in enumerate(parts):
        for t in range(steps):
            at = j * pad_rows + t * rows
            gathered[at : at + rows, :] = ref[t].astype(F32)
        at = j * pad_rows + steps * rows
        gathered[at : (j + 1) * pad_rows, :] = jnp.zeros((pad_rows - steps * rows, width), F32)
    result = dot(
        gathered[...].astype(BF16), down_ref[...].reshape(resident * rank, width), ((1,), (1,))
    )
    for ref in earlier:
        out_ref[: ref.shape[0], :] = ref[...]
    out_ref[out_ref.shape[0] - result.shape[0] :, :] = result


def first_kernel(out_ref):
    out_ref[...] = jnp.zeros_like(out_ref)


def own_rank_kernel(own_ref, down_ref, table_ref, _, out_ref, kept_ref, split_ref, gathered):
    width = table_ref.shape[1]
    rest = table_ref[...]
    for i in range(3):
        part = rest.astype(BF16)
        split_ref[:, i * width : (i + 1) * width] = part
        rest = rest - part.astype(F32)
    rank_kernel(1, own_ref, down_ref, out_ref, gathered)
    kept_ref[...] = down_ref[...]


def copy_kernel(in_ref, _, out_ref):
    out_ref[...] = in_ref[...]


def query_kernel(parts, block, *refs):
    rank_refs = refs[:parts]
    up_ref, base_ref, table_ref = refs[parts : parts + 3]
    out_ref, facts_ref, angles_ref = refs[-3:]
    resident, rank, _ = up_ref.shape
    steps, rows, width = out_ref.shape
    pad_rows = facts_ref.shape[0]
    facts_ref[...] = jnp.zeros_like(facts_ref)
    for t in range(steps):
        facts_ref[t * rows : (t + 1) * rows, :] = base_ref[t, :, width:].astype(F32)
    ids = facts_ref[:, LANES // 2 : LANES // 2 + 1].astype(jnp.int32)
    shape = (pad_rows, table_ref.shape[0])
    step = lax.broadcasted_iota(jnp.int32, shape, 0) // rows
    place = (lax.broadcasted_iota(jnp.int32, shape, 1) - step).astype(F32)
    picked = (place == facts_ref[:, 0:1]).astype(F32).astype(BF16)
    found = dot(picked, table_ref[...], ((1,), (0,)))
    angles_ref[...] = found[:, : 2 * LANES] + found[:, 2 * LANES : 4 * LANES] + found[:, 4 * LANES :]
    ranks = functools.reduce(
        jnp.add, [ref[block * pad_rows : (block + 1) * pad_rows, :] for ref in rank_refs]
    )
    lane = lax.broadcasted_iota(jnp.int32, ranks.shape, 1)
    owner = lax.axis_index("adapter") * resident + lane // rank
    chosen = jnp.where(owner == ids, ranks, 0.0).astype(BF16)
    correction = dot(chosen, up_ref[...].reshape(resident * rank, width), ((1,), (0,)))
    for t in range(steps):
        cos_part = angles_ref[t * rows : (t + 1) * rows, :LANES]
        sin_part = angles_ref[t * rows : (t + 1) * rows, LANES:]
        for h in range(width // HEAD_SIZE):
            at = slice(h * HEAD_SIZE, (h + 1) * HEAD_SIZE)
            piece = base_ref[t, :, at].astype(F32) + correction[t * rows : (t + 1) * rows, at]
            turned = piece * cos_part + pltpu.roll(piece, HEAD_SIZE // 2, 1) * sin_part
            out_ref[t, :, at] = turned.astype(BF16)


def pick_kernel(adapters, resident, *refs):
    queries = refs[:adapters]
    base_ref, _, out_ref, meta_ref = refs[adapters:]
    meta_ref[...] = base_ref[0, :, out_ref.shape[2] :].astype(F32).astype(jnp.int32)
    owner = meta_ref[:, LANES // 2 : LANES // 2 + 1] // resident
    x = lax.axis_index("adapter")
    for t in range(out_ref.shape[0]):
        picked = queries[0][t].astype(F32)
        for j in range(1, adapters):
            picked = jnp.where(owner == peer(x, j, adapters), queries[j][t].astype(F32), picked)
        out_ref[t] = picked.astype(BF16)


def load_queries(query_ref, rows_ref):
    steps, rows, _ = query_ref.shape
    rows_ref[...] = jnp.zeros_like(rows_ref)
    for t in range(steps):
        rows_ref[t * rows : (t + 1) * rows, :] = query_ref[t].astype(F32)


def group_queries(rows_ref, first, group):
    pieces = [
        rows_ref[:, first + g * HEAD_SIZE : first + (g + 1) * HEAD_SIZE] for g in range(group)
    ]
    return jnp.concatenate(pieces, axis=0).astype(BF16)


def attend(queries, keys, values, scale):
    scores = []
    for query, parts in zip(queries, keys):
        found = []
        for key, bias in parts:
            part = dot(query, key, ((1,), (1,)))
            found.append(part if bias is None else part + bias)
        scores.append(found[0] if len(found) == 1 else jnp.concatenate(found, axis=1))
    peaks = [jnp.max(score, axis=1, keepdims=True) * scale for score in scores]
    weights = [jnp.exp2(s * scale - p).astype(BF16) for s, p in zip(scores, peaks)]
    for weight, peak, parts in zip(weights, peaks, values):
        value = parts[0] if len(parts) == 1 else jnp.concatenate(parts, axis=0)
        ones = jnp.ones((value.shape[0], LANES), BF16)
        summed = dot(weight, jnp.concatenate([value, ones], axis=1), ((1,), (0,)))
        total = summed[:, HEAD_SIZE:]
        yield summed[:, :HEAD_SIZE] * (1.0 / total), peak + jnp.log2(total)


def split_stat(stat, heads):
    first = stat.astype(BF16).astype(F32)
    second = (stat - first).astype(BF16).astype(F32)
    third = stat - first - second
    lane = lax.broadcasted_iota(jnp.int32, stat.shape, 1)
    out = jnp.where(lane < heads, first, 0.0)
    out = jnp.where((lane >= heads) & (lane < 2 * heads), pltpu.roll(second, heads, 1), out)
    out = jnp.where(
        (lane >= 2 * heads) & (lane < 3 * heads), pltpu.roll(third, 2 * heads, 1), out
    )
    return out


def far_kernel(scale, query_ref, kv_ref, out_ref, rows_ref, kept, stats_ref):
    steps, rows, width = query_ref.shape
    heads = width // HEAD_SIZE
    kv_heads = kv_ref.shape[2] // HEAD_SIZE
    group = heads // kv_heads
    cut = rows_ref.shape[0]
    load_queries(query_ref, rows_ref)
    columns = [slice(kv * HEAD_SIZE, (kv + 1) * HEAD_SIZE) for kv in range(kv_heads)]
    found = attend(
        [group_queries(rows_ref, kv * group * HEAD_SIZE, group) for kv in range(kv_heads)],
        [[(kv_ref[0, :, at], None)] for at in columns],
        [[kv_ref[1, :, at]] for at in columns],
        scale,
    )
    stats_ref[...] = split_stat(collect(found, kept, cut, group), heads)
    for t in range(steps):
        at = t * rows
        out_ref[t, :, :width] = kept[at : at + rows, :].astype(BF16)
        out_ref[t, :, width:] = stats_ref[at : at + rows, :].astype(BF16)


def collect(found, kept, cut, group):
    lane = lax.broadcasted_iota(jnp.int32, (cut, LANES), 1)
    stats = jnp.zeros((cut, LANES), F32)
    for kv, (result, level) in enumerate(found):
        for g in range(group):
            head = kv * group + g
            kept[:, head * HEAD_SIZE : (head + 1) * HEAD_SIZE] = result[g * cut : (g + 1) * cut]
            stats = jnp.where(lane == head, level[g * cut : (g + 1) * cut], stats)
    return stats


def near_kernel(scale, query_ref, kv_ref, suffix_ref, fresh_ref, meta_ref, *refs):
    own_ref, level_ref, rows_ref, kept, stats, fresh_rows, length_rows = refs
    load_queries(query_ref, rows_ref)
    steps, rows, width = query_ref.shape
    heads = width // HEAD_SIZE
    kv_heads = kv_ref.shape[2] // HEAD_SIZE
    group = heads // kv_heads
    cut = rows_ref.shape[0]
    fresh_rows[...] = jnp.zeros_like(fresh_rows)
    length_rows[...] = jnp.zeros_like(length_rows)
    for t in range(steps):
        length_rows[t * rows : (t + 1) * rows, :] = meta_ref[...]
        for part in range(2):
            fresh_rows[part, t * rows : (t + 1) * rows, :] = fresh_ref[part, t].astype(F32)
    slots = suffix_ref.shape[2]
    suffix_count = rows * slots
    shape = (cut, suffix_count + fresh_rows.shape[1])
    token = lax.broadcasted_iota(jnp.int32, shape, 0)
    column = lax.broadcasted_iota(jnp.int32, shape, 1)
    token_row, token_step = token % rows, token // rows
    fresh_at = column - suffix_count
    in_suffix = (column < suffix_count) & (column // slots == token_row)
    in_suffix &= column % slots < length_rows[:, 0:1]
    in_fresh = (column >= suffix_count) & (fresh_at % rows == token_row)
    in_fresh &= fresh_at // rows <= token_step
    bias = jnp.where(in_suffix | in_fresh, 0.0, MASKED)
    bias = jnp.concatenate([bias] * group, axis=0)
    columns = [slice(kv * HEAD_SIZE, (kv + 1) * HEAD_SIZE) for kv in range(kv_heads)]

    def local(part, at):
        pieces = [suffix_ref[part, r, :, at] for r in range(rows)]
        return jnp.concatenate(pieces + [fresh_rows[part, :, at].astype(BF16)], axis=0)

    found = attend(
        [group_queries(rows_ref, kv * group * HEAD_SIZE, group) for kv in range(kv_heads)],
        [[(kv_ref[0, :, at], None), (local(0, at), bias)] for at in columns],
        [[kv_ref[1, :, at], local(1, at)] for at in columns],
        scale,
    )
    stats[...] = collect(found, kept, cut, group)
    for t in range(steps):
        own_ref[t] = kept[t * rows : (t + 1) * rows, :]
        level_ref[t] = stats[t * rows : (t + 1) * rows, :]


def message_levels(packed, heads):
    count = packed.shape[1]
    return (
        packed + pltpu.roll(packed, count - heads, 1) + pltpu.roll(packed, count - 2 * heads, 1)
    )


def mix(own_ref, level_ref, arrived, store, finish=None):
    steps, _, width = own_ref.shape
    heads = width // HEAD_SIZE
    shares, levels = [], []
    for t in range(steps):
        parts = [level_ref[t]]
        for ref in arrived:
            parts.append(message_levels(ref[t, :, width:].astype(F32), heads))
        highest = functools.reduce(jnp.maximum, parts)
        weights = [jnp.exp2(part - highest) for part in parts]
        total = functools.reduce(jnp.add, weights)
        inverse = 1.0 / total
        shares.append([weight * inverse for weight in weights])
        levels.append(highest + jnp.log2(total))
    quarter = heads // 4 if heads % 4 == 0 else heads
    for h in range(heads):
        at = slice(h * HEAD_SIZE, (h + 1) * HEAD_SIZE)
        for t in range(steps):
            mixed = own_ref[t, :, at] * shares[t][0][:, h : h + 1]
            for ref, share in zip(arrived, shares[t][1:]):
                mixed += ref[t, :, at].astype(F32) * share[:, h : h + 1]
            store(t, at, mixed)
        if finish and (h + 1) % quarter == 0:
            finish(slice((h + 1 - quarter) * HEAD_SIZE, (h + 1) * HEAD_SIZE))
    return levels


def blend_kernel(*refs):
    arrived = refs[:-4]
    own_ref, level_ref, out_ref, out_level_ref = refs[-4:]

    def store(t, at, mixed):
        out_ref[t, :, at] = mixed

    for t, level in enumerate(mix(own_ref, level_ref, arrived, store)):
        out_level_ref[t] = level


def merge_kernel(messages, adapters, *refs):
    arrived = refs[:messages]
    own_ref, level_ref = refs[messages : messages + 2]
    downs = refs[2 + messages : 2 + messages + adapters]
    meta_ref, out_ref, rank_ref, rows_ref, ids_ref = refs[2 + messages + adapters :]
    steps, rows, _ = own_ref.shape
    resident, rank, _ = downs[0].shape
    depth = resident * rank
    x = lax.axis_index("adapter")
    rows_ref[...] = jnp.zeros_like(rows_ref)
    ids_ref[...] = jnp.zeros_like(ids_ref)
    for t in range(steps):
        ids_ref[t * rows : (t + 1) * rows, :] = meta_ref[...]
    products = []

    def store(t, at, mixed):
        out_ref[t, :, at] = mixed.astype(BF16)
        rows_ref[t * rows : (t + 1) * rows, at] = mixed

    def finish(at):
        factors = [down[u, :, at] for down in downs for u in range(resident)]
        products.append(
            dot(rows_ref[:, at].astype(BF16), jnp.concatenate(factors, axis=0), ((1,), (1,)))
        )

    mix(own_ref, level_ref, arrived, store, finish)
    result = functools.reduce(jnp.add, products)
    lane = lax.broadcasted_iota(jnp.int32, result.shape, 1)
    owner = peer(x, lane // depth, adapters) * resident + lane % depth // rank
    rank_ref[...] = jnp.where(owner == ids_ref[:, LANES // 2 : LANES // 2 + 1], result, 0.0)


def up_kernel(parts, adapters, *refs):
    ranks = refs[:parts]
    ups = refs[parts : parts + adapters]
    attended_ref, attended_hbm, out_hbm, out_ref, sems = refs[parts + adapters :]
    copies = [pltpu.make_async_copy(attended_ref, attended_hbm, sems.at[4])]
    copies[0].start()
    steps, rows, width = out_ref.shape
    resident = ups[0].shape[0]
    chosen = functools.reduce(jnp.add, [ref[...] for ref in ranks]).astype(BF16)
    quarter = width // 4
    for i in range(4):
        at = slice(i * quarter, (i + 1) * quarter)
        factors = jnp.concatenate([up[u, :, at] for up in ups for u in range(resident)], axis=0)
        result = dot(chosen, factors, ((1,), (0,)))
        for t in range(steps):
            out_ref[t, :, at] = result[t * rows : (t + 1) * rows].astype(BF16)
        copy = pltpu.make_async_copy(out_ref.at[:, :, at], out_hbm.at[:, :, at], sems.at[i])
        copy.start()
        copies.append(copy)
    for copy in copies:
        copy.wait()


def rope_table(slots, first_position):
    half_dim = HEAD_SIZE // 2
    frequency = rope_base ** (-2.0 * jnp.arange(half_dim, dtype=F32) / HEAD_SIZE)
    position = (first_position + jnp.arange(slots, dtype=jnp.int32)).astype(F32)
    angles = position[:, None] * frequency
    cos_part, sin_part = jnp.cos(angles), jnp.sin(angles)
    return jnp.concatenate([cos_part, cos_part, -sin_part, sin_part], axis=1)


def on_device(
    hidden,
    base_query_rows,
    fresh_key_value,
    suffix_key_value,
    suffix_length,
    row_adapter_index,
    prompt_key_value,
    query_down_factors,
    query_up_factors,
    output_down_factors,
    output_up_factors,
):
    rows, steps, width = hidden.shape
    seq_count, adapters, halves = (lax.axis_size(name) for name in ("seq", "adapter", "head"))
    slots = suffix_key_value.shape[2]
    resident, rank, _ = query_down_factors.shape
    depth = resident * rank
    tokens = rows * steps
    pad_rows = -(-tokens // 16) * 16
    heads = width // HEAD_SIZE
    kv_heads = prompt_key_value.shape[2] // HEAD_SIZE
    group = heads // kv_heads
    scale = math.log2(math.e) / math.sqrt(HEAD_SIZE)
    stat_lanes = -(-3 * heads // LANES) * LANES
    hidden = hidden.transpose(1, 0, 2)
    lane = lax.broadcasted_iota(jnp.int32, (steps, rows, width + LANES), 2)
    facts = jnp.where(lane < width + LANES // 2, suffix_length[:, None], row_adapter_index)
    base = jnp.pad(base_query_rows.transpose(1, 0, 2), ((0, 0), (0, 0), (0, LANES)))
    base = jnp.where(lane < width, base, facts.astype(BF16))
    fresh = fresh_key_value.transpose(0, 2, 1, 3)

    own_rows = jax.ShapeDtypeStruct((pad_rows, depth), F32)
    factors = jax.ShapeDtypeStruct(query_down_factors.shape, BF16)
    first = call(first_kernel, jax.ShapeDtypeStruct((8, LANES), F32), (), flops=1 << 34)
    table_slots = -(-(slots + steps) // 16) * 16
    table = rope_table(table_slots, prompt_key_value.shape[1] * seq_count)
    own_ranks, own_down, table = call(
        own_rank_kernel,
        (own_rows, factors, jax.ShapeDtypeStruct((table_slots, 6 * LANES), BF16)),
        (hidden, query_down_factors, table, first),
        scratch=[pltpu.VMEM((pad_rows, width), F32)],
    )
    hidden_of = [fetch(hidden, "adapter", j) for j in range(1, adapters)]
    ranks = call(
        functools.partial(rank_kernel, adapters - 1),
        jax.ShapeDtypeStruct((adapters * pad_rows, depth), F32),
        (*hidden_of, own_down, own_ranks),
        scratch=[pltpu.VMEM(((adapters - 1) * pad_rows, width), F32)],
    )
    rank_parts = [ranks] + [fetch(ranks, "head", j) for j in range(1, halves)]
    own_up = call(
        copy_kernel,
        jax.ShapeDtypeStruct(query_up_factors.shape, BF16),
        (query_up_factors, ranks),
    )
    block_queries = []
    for j in reversed(range(adapters)):
        block_base = fetch(base, "adapter", j) if j else base
        block_queries.insert(
            0,
            call(
                functools.partial(query_kernel, halves, j),
                jax.ShapeDtypeStruct((steps, rows, width), BF16),
                (
                    *rank_parts,
                    own_up,
                    block_base,
                    table,
                    *block_queries[:1],
                ),
                scratch=[
                    pltpu.VMEM((pad_rows, LANES), F32),
                    pltpu.VMEM((pad_rows, 2 * LANES), F32),
                ],
            ),
        )
    arrived = [send(part, "adapter", j) for j, part in enumerate(block_queries) if j]
    output_down_factors, output_up_factors, token = lax.optimization_barrier(
        (output_down_factors, output_up_factors, block_queries[0][0, :, :LANES])
    )
    queries, meta = call(
        functools.partial(pick_kernel, adapters, resident),
        (
            jax.ShapeDtypeStruct((steps, rows, width), BF16),
            jax.ShapeDtypeStruct((rows, LANES), jnp.int32),
        ),
        (block_queries[0], *arrived, base, token),
        flops=1 << 36,
    )
    message = jax.ShapeDtypeStruct((steps, rows, width + stat_lanes), BF16)
    query_scratch = [
        pltpu.VMEM((pad_rows, width), F32),
        pltpu.VMEM((pad_rows, width), F32),
        pltpu.VMEM((pad_rows, LANES), F32),
    ]
    piece_of = {0: queries}
    for k in range(1, seq_count):
        piece_of[k] = fetch(piece_of[k - 1], "seq", 1) if k % 2 else fetch(queries, "seq", k)
    order = list(range(2, seq_count)) + [1]
    messages = []
    for k in order:
        messages.append(
            call(
                functools.partial(far_kernel, scale),
                message,
                (piece_of[k], prompt_key_value),
                scratch=query_scratch,
            )
        )
    fresh_slots = -(-tokens // LANES) * LANES
    part_shapes = (
        jax.ShapeDtypeStruct((steps, rows, width), F32),
        jax.ShapeDtypeStruct((steps, rows, LANES), F32),
    )
    own, level = call(
        functools.partial(near_kernel, scale),
        part_shapes,
        (queries, prompt_key_value, suffix_key_value, fresh, meta),
        scratch=query_scratch
        + [
            pltpu.VMEM((2, fresh_slots, fresh.shape[3]), F32),
            pltpu.VMEM((pad_rows, LANES), jnp.int32),
        ],
    )
    output_downs = [output_down_factors] + [
        fetch(output_down_factors, "adapter", j) for j in range(1, adapters)
    ]
    output_ups = [output_up_factors] + [
        fetch(output_up_factors, "adapter", j) for j in range(1, adapters)
    ]
    partials = [send(part, "seq", k) for part, k in zip(messages, order)]
    last = max(seq_count - 3, 0)
    early, partials = partials[:last] + partials[last + 1 :], partials[last : last + 1]
    if early:
        own, level = call(blend_kernel, part_shapes, (*early, own, level))
    attended, out_rank = call(
        functools.partial(merge_kernel, len(partials), adapters),
        (
            jax.ShapeDtypeStruct((steps, rows, width), BF16),
            jax.ShapeDtypeStruct((pad_rows, adapters * depth), F32),
        ),
        (*partials, own, level, *output_downs, meta),
        scratch=[
            pltpu.VMEM((pad_rows, width), F32),
            pltpu.VMEM((pad_rows, LANES), jnp.int32),
        ],
    )
    out_ranks = [out_rank] + [fetch(out_rank, "head", j) for j in range(1, halves)]
    attended, adapted = call(
        functools.partial(up_kernel, halves, adapters),
        (jax.ShapeDtypeStruct((steps, rows, width), BF16),) * 2,
        (*out_ranks, *output_ups, attended),
        scratch=[pltpu.VMEM((steps, rows, width), BF16), pltpu.SemaphoreType.DMA((5,))],
        out_specs=(pl.BlockSpec(memory_space=pl.ANY),) * 2,
    )
    return attended.transpose(1, 0, 2), adapted.transpose(1, 0, 2)


def solution(mesh):
    rows = ("groups", "seq", "adapter")
    factors = P(("groups", "adapter"), None, "head")
    placed = (
        P(rows, None, "head"),
        P(rows, None, "head"),
        P(None, rows, None, "head"),
        P(None, rows, None, "head"),
        P(rows),
        P(rows, None),
        P(None, ("groups", "seq"), "head"),
        factors,
        factors,
        factors,
        factors,
    )
    return jax.shard_map(
        on_device,
        mesh=mesh,
        in_specs=placed,
        out_specs=(P(rows, None, "head"), P(rows, None, "head")),
        check_vma=False,
    )
```

```python
import functools
import math

import jax
import jax.numpy as jnp
from jax import lax
from jax.experimental import pallas as pl
from jax.experimental.pallas import tpu as pltpu
from jax.sharding import PartitionSpec as P

HEAD_SIZE = 128
LANES = 128
rope_base = 1000000.0
MASKED = -1e30
VMEM_BYTES = 8 << 20

VMEM = pl.BlockSpec(memory_space=pltpu.VMEM)
F32 = jnp.float32
BF16 = jnp.bfloat16


def peer(index, offset, size):
    if size & (size - 1) == 0:
        return index ^ offset
    return (index + offset) % size


def fetch(value, axis, offset):
    size = lax.axis_size(axis)
    return lax.ppermute(value, axis, [(peer(i, offset, size), i) for i in range(size)])


def send(value, axis, offset):
    size = lax.axis_size(axis)
    return lax.ppermute(value, axis, [(i, peer(i, offset, size)) for i in range(size)])


def dot(left, right, contract):
    return lax.dot_general(left, right, (contract, ((), ())), preferred_element_type=F32)


def call(kernel, out_shape, args, specs=None, scratch=(), flops=1 << 20, out_specs=None):
    return pl.pallas_call(
        kernel,
        out_shape=out_shape,
        in_specs=specs or [VMEM] * len(args),
        out_specs=out_specs or jax.tree.map(lambda unused: VMEM, out_shape),
        scratch_shapes=scratch,
        compiler_params=pltpu.CompilerParams(vmem_limit_bytes=VMEM_BYTES),
        cost_estimate=pl.CostEstimate(flops=flops, bytes_accessed=1 << 20, transcendentals=0),
    )(*args)


def rank_kernel(count, *refs):
    parts = refs[:count]
    down_ref = refs[count]
    earlier, out_ref, gathered = refs[count + 1 : -2], *refs[-2:]
    steps, rows, width = parts[0].shape
    resident, rank, _ = down_ref.shape
    pad_rows = gathered.shape[0] // count
    for j, ref in enumerate(parts):
        for t in range(steps):
            at = j * pad_rows + t * rows
            gathered[at : at + rows, :] = ref[t].astype(F32)
        at = j * pad_rows + steps * rows
        gathered[at : (j + 1) * pad_rows, :] = jnp.zeros((pad_rows - steps * rows, width), F32)
    result = dot(
        gathered[...].astype(BF16), down_ref[...].reshape(resident * rank, width), ((1,), (1,))
    )
    for ref in earlier:
        out_ref[: ref.shape[0], :] = ref[...]
    out_ref[out_ref.shape[0] - result.shape[0] :, :] = result


def first_kernel(out_ref):
    out_ref[...] = jnp.zeros_like(out_ref)


def own_rank_kernel(own_ref, down_ref, table_ref, _, out_ref, kept_ref, split_ref, gathered):
    width = table_ref.shape[1]
    rest = table_ref[...]
    for i in range(3):
        part = rest.astype(BF16)
        split_ref[:, i * width : (i + 1) * width] = part
        rest = rest - part.astype(F32)
    rank_kernel(1, own_ref, down_ref, out_ref, gathered)
    kept_ref[...] = down_ref[...]


def copy_kernel(in_ref, _, out_ref):
    out_ref[...] = in_ref[...]


def query_kernel(parts, block, *refs):
    rank_refs = refs[:parts]
    up_ref, base_ref, table_ref = refs[parts : parts + 3]
    out_ref, facts_ref, angles_ref = refs[-3:]
    resident, rank, _ = up_ref.shape
    steps, rows, width = out_ref.shape
    pad_rows = facts_ref.shape[0]
    facts_ref[...] = jnp.zeros_like(facts_ref)
    for t in range(steps):
        facts_ref[t * rows : (t + 1) * rows, :] = base_ref[t, :, width:].astype(F32)
    ids = facts_ref[:, LANES // 2 : LANES // 2 + 1].astype(jnp.int32)
    shape = (pad_rows, table_ref.shape[0])
    step = lax.broadcasted_iota(jnp.int32, shape, 0) // rows
    place = (lax.broadcasted_iota(jnp.int32, shape, 1) - step).astype(F32)
    picked = (place == facts_ref[:, 0:1]).astype(F32).astype(BF16)
    found = dot(picked, table_ref[...], ((1,), (0,)))
    angles_ref[...] = found[:, : 2 * LANES] + found[:, 2 * LANES : 4 * LANES] + found[:, 4 * LANES :]
    ranks = functools.reduce(
        jnp.add, [ref[block * pad_rows : (block + 1) * pad_rows, :] for ref in rank_refs]
    )
    lane = lax.broadcasted_iota(jnp.int32, ranks.shape, 1)
    owner = lax.axis_index("adapter") * resident + lane // rank
    chosen = jnp.where(owner == ids, ranks, 0.0).astype(BF16)
    correction = dot(chosen, up_ref[...].reshape(resident * rank, width), ((1,), (0,)))
    for t in range(steps):
        cos_part = angles_ref[t * rows : (t + 1) * rows, :LANES]
        sin_part = angles_ref[t * rows : (t + 1) * rows, LANES:]
        for h in range(width // HEAD_SIZE):
            at = slice(h * HEAD_SIZE, (h + 1) * HEAD_SIZE)
            piece = base_ref[t, :, at].astype(F32) + correction[t * rows : (t + 1) * rows, at]
            turned = piece * cos_part + pltpu.roll(piece, HEAD_SIZE // 2, 1) * sin_part
            out_ref[t, :, at] = turned.astype(BF16)


def pick_kernel(adapters, resident, *refs):
    queries = refs[:adapters]
    base_ref, _, out_ref, meta_ref = refs[adapters:]
    meta_ref[...] = base_ref[0, :, out_ref.shape[2] :].astype(F32).astype(jnp.int32)
    owner = meta_ref[:, LANES // 2 : LANES // 2 + 1] // resident
    x = lax.axis_index("adapter")
    for t in range(out_ref.shape[0]):
        picked = queries[0][t].astype(F32)
        for j in range(1, adapters):
            picked = jnp.where(owner == peer(x, j, adapters), queries[j][t].astype(F32), picked)
        out_ref[t] = picked.astype(BF16)


def load_queries(query_ref, rows_ref):
    steps, rows, _ = query_ref.shape
    rows_ref[...] = jnp.zeros_like(rows_ref)
    for t in range(steps):
        rows_ref[t * rows : (t + 1) * rows, :] = query_ref[t].astype(F32)


def group_queries(rows_ref, first, group):
    pieces = [
        rows_ref[:, first + g * HEAD_SIZE : first + (g + 1) * HEAD_SIZE] for g in range(group)
    ]
    return jnp.concatenate(pieces, axis=0).astype(BF16)


def attend(queries, keys, values, scale):
    scores = []
    for query, parts in zip(queries, keys):
        found = []
        for key, bias in parts:
            part = dot(query, key, ((1,), (1,)))
            found.append(part if bias is None else part + bias)
        scores.append(found[0] if len(found) == 1 else jnp.concatenate(found, axis=1))
    peaks = [jnp.max(score, axis=1, keepdims=True) * scale for score in scores]
    weights = [jnp.exp2(s * scale - p).astype(BF16) for s, p in zip(scores, peaks)]
    for weight, peak, parts in zip(weights, peaks, values):
        value = parts[0] if len(parts) == 1 else jnp.concatenate(parts, axis=0)
        ones = jnp.ones((value.shape[0], LANES), BF16)
        summed = dot(weight, jnp.concatenate([value, ones], axis=1), ((1,), (0,)))
        total = summed[:, HEAD_SIZE:]
        yield summed[:, :HEAD_SIZE] * (1.0 / total), peak + jnp.log2(total)


def split_stat(stat, heads):
    first = stat.astype(BF16).astype(F32)
    second = (stat - first).astype(BF16).astype(F32)
    third = stat - first - second
    lane = lax.broadcasted_iota(jnp.int32, stat.shape, 1)
    out = jnp.where(lane < heads, first, 0.0)
    out = jnp.where((lane >= heads) & (lane < 2 * heads), pltpu.roll(second, heads, 1), out)
    out = jnp.where(
        (lane >= 2 * heads) & (lane < 3 * heads), pltpu.roll(third, 2 * heads, 1), out
    )
    return out


def far_kernel(scale, query_ref, kv_ref, *refs):
    out_ref, rows_ref, kept, stats_ref = refs[-4:]
    steps, rows, width = query_ref.shape
    heads = width // HEAD_SIZE
    kv_heads = kv_ref.shape[2] // HEAD_SIZE
    group = heads // kv_heads
    cut = rows_ref.shape[0]
    load_queries(query_ref, rows_ref)
    columns = [slice(kv * HEAD_SIZE, (kv + 1) * HEAD_SIZE) for kv in range(kv_heads)]
    found = attend(
        [group_queries(rows_ref, kv * group * HEAD_SIZE, group) for kv in range(kv_heads)],
        [[(kv_ref[0, :, at], None)] for at in columns],
        [[kv_ref[1, :, at]] for at in columns],
        scale,
    )
    stats_ref[...] = split_stat(collect(found, kept, cut, group), heads)
    for t in range(steps):
        at = t * rows
        out_ref[t, :, :width] = kept[at : at + rows, :].astype(BF16)
        out_ref[t, :, width:] = stats_ref[at : at + rows, :].astype(BF16)


def collect(found, kept, cut, group):
    lane = lax.broadcasted_iota(jnp.int32, (cut, LANES), 1)
    stats = jnp.zeros((cut, LANES), F32)
    for kv, (result, level) in enumerate(found):
        for g in range(group):
            head = kv * group + g
            kept[:, head * HEAD_SIZE : (head + 1) * HEAD_SIZE] = result[g * cut : (g + 1) * cut]
            stats = jnp.where(lane == head, level[g * cut : (g + 1) * cut], stats)
    return stats


def near_kernel(scale, query_ref, kv_ref, suffix_ref, fresh_ref, meta_ref, *refs):
    own_ref, level_ref, rows_ref, kept, stats, fresh_rows, length_rows = refs
    load_queries(query_ref, rows_ref)
    steps, rows, width = query_ref.shape
    heads = width // HEAD_SIZE
    kv_heads = kv_ref.shape[2] // HEAD_SIZE
    group = heads // kv_heads
    cut = rows_ref.shape[0]
    fresh_rows[...] = jnp.zeros_like(fresh_rows)
    length_rows[...] = jnp.zeros_like(length_rows)
    for t in range(steps):
        length_rows[t * rows : (t + 1) * rows, :] = meta_ref[...]
        for part in range(2):
            fresh_rows[part, t * rows : (t + 1) * rows, :] = fresh_ref[part, t].astype(F32)
    slots = suffix_ref.shape[2]
    suffix_count = rows * slots
    shape = (cut, suffix_count + fresh_rows.shape[1])
    token = lax.broadcasted_iota(jnp.int32, shape, 0)
    column = lax.broadcasted_iota(jnp.int32, shape, 1)
    token_row, token_step = token % rows, token // rows
    fresh_at = column - suffix_count
    in_suffix = (column < suffix_count) & (column // slots == token_row)
    in_suffix &= column % slots < length_rows[:, 0:1]
    in_fresh = (column >= suffix_count) & (fresh_at % rows == token_row)
    in_fresh &= fresh_at // rows <= token_step
    bias = jnp.where(in_suffix | in_fresh, 0.0, MASKED)
    bias = jnp.concatenate([bias] * group, axis=0)
    columns = [slice(kv * HEAD_SIZE, (kv + 1) * HEAD_SIZE) for kv in range(kv_heads)]

    def local(part, at):
        pieces = [suffix_ref[part, r, :, at] for r in range(rows)]
        return jnp.concatenate(pieces + [fresh_rows[part, :, at].astype(BF16)], axis=0)

    found = attend(
        [group_queries(rows_ref, kv * group * HEAD_SIZE, group) for kv in range(kv_heads)],
        [[(kv_ref[0, :, at], None), (local(0, at), bias)] for at in columns],
        [[kv_ref[1, :, at], local(1, at)] for at in columns],
        scale,
    )
    stats[...] = collect(found, kept, cut, group)
    for t in range(steps):
        own_ref[t] = kept[t * rows : (t + 1) * rows, :]
        level_ref[t] = stats[t * rows : (t + 1) * rows, :]


def message_levels(packed, heads):
    count = packed.shape[1]
    return (
        packed + pltpu.roll(packed, count - heads, 1) + pltpu.roll(packed, count - 2 * heads, 1)
    )


def mix(own_ref, level_ref, arrived, store, finish=None):
    steps, _, width = own_ref.shape
    heads = width // HEAD_SIZE
    shares, levels = [], []
    for t in range(steps):
        parts = [level_ref[t]]
        for ref in arrived:
            parts.append(message_levels(ref[t, :, width:].astype(F32), heads))
        highest = functools.reduce(jnp.maximum, parts)
        weights = [jnp.exp2(part - highest) for part in parts]
        total = functools.reduce(jnp.add, weights)
        inverse = 1.0 / total
        shares.append([weight * inverse for weight in weights])
        levels.append(highest + jnp.log2(total))
    quarter = heads // 4 if heads % 4 == 0 else heads
    for h in range(heads):
        at = slice(h * HEAD_SIZE, (h + 1) * HEAD_SIZE)
        for t in range(steps):
            mixed = own_ref[t, :, at] * shares[t][0][:, h : h + 1]
            for ref, share in zip(arrived, shares[t][1:]):
                mixed += ref[t, :, at].astype(F32) * share[:, h : h + 1]
            store(t, at, mixed)
        if finish and (h + 1) % quarter == 0:
            finish(slice((h + 1 - quarter) * HEAD_SIZE, (h + 1) * HEAD_SIZE))
    return levels


def blend_kernel(*refs):
    arrived = refs[:-4]
    own_ref, level_ref, out_ref, out_level_ref = refs[-4:]

    def store(t, at, mixed):
        out_ref[t, :, at] = mixed

    for t, level in enumerate(mix(own_ref, level_ref, arrived, store)):
        out_level_ref[t] = level


def merge_kernel(messages, adapters, *refs):
    arrived = refs[:messages]
    own_ref, level_ref = refs[messages : messages + 2]
    downs = refs[2 + messages : 2 + messages + adapters]
    meta_ref, out_ref, rank_ref, rows_ref, ids_ref = refs[2 + messages + adapters :]
    steps, rows, _ = own_ref.shape
    resident, rank, _ = downs[0].shape
    depth = resident * rank
    x = lax.axis_index("adapter")
    rows_ref[...] = jnp.zeros_like(rows_ref)
    ids_ref[...] = jnp.zeros_like(ids_ref)
    for t in range(steps):
        ids_ref[t * rows : (t + 1) * rows, :] = meta_ref[...]
    products = []

    def store(t, at, mixed):
        out_ref[t, :, at] = mixed.astype(BF16)
        rows_ref[t * rows : (t + 1) * rows, at] = mixed

    def finish(at):
        factors = [down[u, :, at] for down in downs for u in range(resident)]
        products.append(
            dot(rows_ref[:, at].astype(BF16), jnp.concatenate(factors, axis=0), ((1,), (1,)))
        )

    mix(own_ref, level_ref, arrived, store, finish)
    result = functools.reduce(jnp.add, products)
    lane = lax.broadcasted_iota(jnp.int32, result.shape, 1)
    owner = peer(x, lane // depth, adapters) * resident + lane % depth // rank
    rank_ref[...] = jnp.where(owner == ids_ref[:, LANES // 2 : LANES // 2 + 1], result, 0.0)


def up_kernel(parts, adapters, *refs):
    ranks = refs[:parts]
    ups = refs[parts : parts + adapters]
    attended_ref, attended_hbm, out_hbm, out_ref, sems = refs[parts + adapters :]
    copies = [pltpu.make_async_copy(attended_ref, attended_hbm, sems.at[4])]
    copies[0].start()
    steps, rows, width = out_ref.shape
    resident = ups[0].shape[0]
    chosen = functools.reduce(jnp.add, [ref[...] for ref in ranks]).astype(BF16)
    quarter = width // 4
    for i in range(4):
        at = slice(i * quarter, (i + 1) * quarter)
        factors = jnp.concatenate([up[u, :, at] for up in ups for u in range(resident)], axis=0)
        result = dot(chosen, factors, ((1,), (0,)))
        for t in range(steps):
            out_ref[t, :, at] = result[t * rows : (t + 1) * rows].astype(BF16)
        copy = pltpu.make_async_copy(out_ref.at[:, :, at], out_hbm.at[:, :, at], sems.at[i])
        copy.start()
        copies.append(copy)
    for copy in copies:
        copy.wait()


def rope_table(slots, first_position):
    half_dim = HEAD_SIZE // 2
    frequency = rope_base ** (-2.0 * jnp.arange(half_dim, dtype=F32) / HEAD_SIZE)
    position = (first_position + jnp.arange(slots, dtype=jnp.int32)).astype(F32)
    angles = position[:, None] * frequency
    cos_part, sin_part = jnp.cos(angles), jnp.sin(angles)
    return jnp.concatenate([cos_part, cos_part, -sin_part, sin_part], axis=1)


def on_device(
    hidden,
    base_query_rows,
    fresh_key_value,
    suffix_key_value,
    suffix_length,
    row_adapter_index,
    prompt_key_value,
    query_down_factors,
    query_up_factors,
    output_down_factors,
    output_up_factors,
):
    rows, steps, width = hidden.shape
    seq_count, adapters, halves = (lax.axis_size(name) for name in ("seq", "adapter", "head"))
    slots = suffix_key_value.shape[2]
    resident, rank, _ = query_down_factors.shape
    depth = resident * rank
    tokens = rows * steps
    pad_rows = -(-tokens // 16) * 16
    heads = width // HEAD_SIZE
    kv_heads = prompt_key_value.shape[2] // HEAD_SIZE
    group = heads // kv_heads
    scale = math.log2(math.e) / math.sqrt(HEAD_SIZE)
    stat_lanes = -(-3 * heads // LANES) * LANES
    hidden = hidden.transpose(1, 0, 2)
    lane = lax.broadcasted_iota(jnp.int32, (steps, rows, width + LANES), 2)
    facts = jnp.where(lane < width + LANES // 2, suffix_length[:, None], row_adapter_index)
    base = jnp.pad(base_query_rows.transpose(1, 0, 2), ((0, 0), (0, 0), (0, LANES)))
    base = jnp.where(lane < width, base, facts.astype(BF16))
    fresh = fresh_key_value.transpose(0, 2, 1, 3)

    own_rows = jax.ShapeDtypeStruct((pad_rows, depth), F32)
    factors = jax.ShapeDtypeStruct(query_down_factors.shape, BF16)
    first = call(first_kernel, jax.ShapeDtypeStruct((8, LANES), F32), (), flops=1 << 34)
    table_slots = -(-(slots + steps) // 16) * 16
    table = rope_table(table_slots, prompt_key_value.shape[1] * seq_count)
    own_ranks, own_down, table = call(
        own_rank_kernel,
        (own_rows, factors, jax.ShapeDtypeStruct((table_slots, 6 * LANES), BF16)),
        (hidden, query_down_factors, table, first),
        scratch=[pltpu.VMEM((pad_rows, width), F32)],
    )
    hidden_of = [fetch(hidden, "adapter", j) for j in range(1, adapters)]
    ranks = call(
        functools.partial(rank_kernel, adapters - 1),
        jax.ShapeDtypeStruct((adapters * pad_rows, depth), F32),
        (*hidden_of, own_down, own_ranks),
        scratch=[pltpu.VMEM(((adapters - 1) * pad_rows, width), F32)],
    )
    rank_parts = [ranks] + [fetch(ranks, "head", j) for j in range(1, halves)]
    own_up = call(
        copy_kernel,
        jax.ShapeDtypeStruct(query_up_factors.shape, BF16),
        (query_up_factors, ranks),
    )
    block_queries = []
    for j in reversed(range(adapters)):
        block_base = fetch(base, "adapter", j) if j else base
        block_queries.insert(
            0,
            call(
                functools.partial(query_kernel, halves, j),
                jax.ShapeDtypeStruct((steps, rows, width), BF16),
                (
                    *rank_parts,
                    own_up,
                    block_base,
                    table,
                    *block_queries[:1],
                ),
                scratch=[
                    pltpu.VMEM((pad_rows, LANES), F32),
                    pltpu.VMEM((pad_rows, 2 * LANES), F32),
                ],
            ),
        )
    arrived = [send(part, "adapter", j) for j, part in enumerate(block_queries) if j]
    output_down_factors, output_up_factors, token = lax.optimization_barrier(
        (output_down_factors, output_up_factors, block_queries[0][0, :, :LANES])
    )
    queries, meta = call(
        functools.partial(pick_kernel, adapters, resident),
        (
            jax.ShapeDtypeStruct((steps, rows, width), BF16),
            jax.ShapeDtypeStruct((rows, LANES), jnp.int32),
        ),
        (block_queries[0], *arrived, base, token),
        flops=1 << 36,
    )
    message = jax.ShapeDtypeStruct((steps, rows, width + stat_lanes), BF16)
    query_scratch = [
        pltpu.VMEM((pad_rows, width), F32),
        pltpu.VMEM((pad_rows, width), F32),
        pltpu.VMEM((pad_rows, LANES), F32),
    ]
    piece_of = {0: queries}
    for k in range(1, seq_count):
        piece_of[k] = fetch(piece_of[k - 1], "seq", 1) if k % 2 else fetch(queries, "seq", k)
    order = [1] + list(range(2, seq_count))
    messages = []
    for k in order:
        messages.append(
            call(
                functools.partial(far_kernel, scale),
                message,
                (piece_of[k], prompt_key_value, *messages[: k == 2]),
                scratch=query_scratch,
            )
        )
    fresh_slots = -(-tokens // LANES) * LANES
    part_shapes = (
        jax.ShapeDtypeStruct((steps, rows, width), F32),
        jax.ShapeDtypeStruct((steps, rows, LANES), F32),
    )
    own, level = call(
        functools.partial(near_kernel, scale),
        part_shapes,
        (queries, prompt_key_value, suffix_key_value, fresh, meta),
        scratch=query_scratch
        + [
            pltpu.VMEM((2, fresh_slots, fresh.shape[3]), F32),
            pltpu.VMEM((pad_rows, LANES), jnp.int32),
        ],
    )
    output_downs = [output_down_factors] + [
        fetch(output_down_factors, "adapter", j) for j in range(1, adapters)
    ]
    output_ups = [output_up_factors] + [
        fetch(output_up_factors, "adapter", j) for j in range(1, adapters)
    ]
    partials = [send(part, "seq", k) for part, k in zip(messages, order)]
    early, partials = partials[:-1], partials[-1:]
    if early:
        own, level = call(blend_kernel, part_shapes, (*early[::-1], own, level))
    attended, out_rank = call(
        functools.partial(merge_kernel, len(partials), adapters),
        (
            jax.ShapeDtypeStruct((steps, rows, width), BF16),
            jax.ShapeDtypeStruct((pad_rows, adapters * depth), F32),
        ),
        (*partials, own, level, *output_downs, meta),
        scratch=[
            pltpu.VMEM((pad_rows, width), F32),
            pltpu.VMEM((pad_rows, LANES), jnp.int32),
        ],
    )
    out_ranks = [out_rank] + [fetch(out_rank, "head", j) for j in range(1, halves)]
    attended, adapted = call(
        functools.partial(up_kernel, halves, adapters),
        (jax.ShapeDtypeStruct((steps, rows, width), BF16),) * 2,
        (*out_ranks, *output_ups, attended),
        scratch=[pltpu.VMEM((steps, rows, width), BF16), pltpu.SemaphoreType.DMA((5,))],
        out_specs=(pl.BlockSpec(memory_space=pl.ANY),) * 2,
    )
    return attended.transpose(1, 0, 2), adapted.transpose(1, 0, 2)


def solution(mesh):
    rows = ("groups", "seq", "adapter")
    factors = P(("groups", "adapter"), None, "head")
    placed = (
        P(rows, None, "head"),
        P(rows, None, "head"),
        P(None, rows, None, "head"),
        P(None, rows, None, "head"),
        P(rows),
        P(rows, None),
        P(None, ("groups", "seq"), "head"),
        factors,
        factors,
        factors,
        factors,
    )
    return jax.shard_map(
        on_device,
        mesh=mesh,
        in_specs=placed,
        out_specs=(P(rows, None, "head"), P(rows, None, "head")),
        check_vma=False,
    )
```

```python
import functools
import math

import jax
import jax.numpy as jnp
from jax import lax
from jax.experimental import pallas as pl
from jax.experimental.pallas import tpu as pltpu
from jax.sharding import PartitionSpec as P

HEAD_SIZE = 128
LANES = 128
rope_base = 1000000.0
MASKED = -1e30
VMEM_BYTES = 8 << 20

VMEM = pl.BlockSpec(memory_space=pltpu.VMEM)
F32 = jnp.float32
BF16 = jnp.bfloat16


def peer(index, offset, size):
    if size & (size - 1) == 0:
        return index ^ offset
    return (index + offset) % size


def fetch(value, axis, offset):
    size = lax.axis_size(axis)
    return lax.ppermute(value, axis, [(peer(i, offset, size), i) for i in range(size)])


def send(value, axis, offset):
    size = lax.axis_size(axis)
    return lax.ppermute(value, axis, [(i, peer(i, offset, size)) for i in range(size)])


def dot(left, right, contract):
    return lax.dot_general(left, right, (contract, ((), ())), preferred_element_type=F32)


def call(kernel, out_shape, args, specs=None, scratch=(), flops=1 << 20, out_specs=None):
    return pl.pallas_call(
        kernel,
        out_shape=out_shape,
        in_specs=specs or [VMEM] * len(args),
        out_specs=out_specs or jax.tree.map(lambda unused: VMEM, out_shape),
        scratch_shapes=scratch,
        compiler_params=pltpu.CompilerParams(vmem_limit_bytes=VMEM_BYTES),
        cost_estimate=pl.CostEstimate(flops=flops, bytes_accessed=1 << 20, transcendentals=0),
    )(*args)


def rank_kernel(count, *refs):
    parts = refs[:count]
    down_ref = refs[count]
    earlier, out_ref, gathered = refs[count + 1 : -2], *refs[-2:]
    steps, rows, width = parts[0].shape
    resident, rank, _ = down_ref.shape
    pad_rows = gathered.shape[0] // count
    for j, ref in enumerate(parts):
        for t in range(steps):
            at = j * pad_rows + t * rows
            gathered[at : at + rows, :] = ref[t].astype(F32)
        at = j * pad_rows + steps * rows
        gathered[at : (j + 1) * pad_rows, :] = jnp.zeros((pad_rows - steps * rows, width), F32)
    result = dot(
        gathered[...].astype(BF16), down_ref[...].reshape(resident * rank, width), ((1,), (1,))
    )
    for ref in earlier:
        out_ref[: ref.shape[0], :] = ref[...]
    out_ref[out_ref.shape[0] - result.shape[0] :, :] = result


def first_kernel(out_ref):
    out_ref[...] = jnp.zeros_like(out_ref)


def own_rank_kernel(own_ref, down_ref, table_ref, _, out_ref, kept_ref, split_ref, gathered):
    width = table_ref.shape[1]
    rest = table_ref[...]
    for i in range(3):
        part = rest.astype(BF16)
        split_ref[:, i * width : (i + 1) * width] = part
        rest = rest - part.astype(F32)
    rank_kernel(1, own_ref, down_ref, out_ref, gathered)
    kept_ref[...] = down_ref[...]


def copy_kernel(in_ref, _, out_ref):
    out_ref[...] = in_ref[...]


def query_kernel(parts, block, *refs):
    rank_refs = refs[:parts]
    up_ref, base_ref, table_ref = refs[parts : parts + 3]
    out_ref, facts_ref, angles_ref = refs[-3:]
    resident, rank, _ = up_ref.shape
    steps, rows, width = out_ref.shape
    pad_rows = facts_ref.shape[0]
    facts_ref[...] = jnp.zeros_like(facts_ref)
    for t in range(steps):
        facts_ref[t * rows : (t + 1) * rows, :] = base_ref[t, :, width:].astype(F32)
    ids = facts_ref[:, LANES // 2 : LANES // 2 + 1].astype(jnp.int32)
    shape = (pad_rows, table_ref.shape[0])
    step = lax.broadcasted_iota(jnp.int32, shape, 0) // rows
    place = (lax.broadcasted_iota(jnp.int32, shape, 1) - step).astype(F32)
    picked = (place == facts_ref[:, 0:1]).astype(F32).astype(BF16)
    found = dot(picked, table_ref[...], ((1,), (0,)))
    angles_ref[...] = found[:, : 2 * LANES] + found[:, 2 * LANES : 4 * LANES] + found[:, 4 * LANES :]
    ranks = functools.reduce(
        jnp.add, [ref[block * pad_rows : (block + 1) * pad_rows, :] for ref in rank_refs]
    )
    lane = lax.broadcasted_iota(jnp.int32, ranks.shape, 1)
    owner = lax.axis_index("adapter") * resident + lane // rank
    chosen = jnp.where(owner == ids, ranks, 0.0).astype(BF16)
    correction = dot(chosen, up_ref[...].reshape(resident * rank, width), ((1,), (0,)))
    for t in range(steps):
        cos_part = angles_ref[t * rows : (t + 1) * rows, :LANES]
        sin_part = angles_ref[t * rows : (t + 1) * rows, LANES:]
        for h in range(width // HEAD_SIZE):
            at = slice(h * HEAD_SIZE, (h + 1) * HEAD_SIZE)
            piece = base_ref[t, :, at].astype(F32) + correction[t * rows : (t + 1) * rows, at]
            turned = piece * cos_part + pltpu.roll(piece, HEAD_SIZE // 2, 1) * sin_part
            out_ref[t, :, at] = turned.astype(BF16)


def pick_kernel(adapters, resident, *refs):
    queries = refs[:adapters]
    base_ref, _, out_ref, meta_ref = refs[adapters:]
    meta_ref[...] = base_ref[0, :, out_ref.shape[2] :].astype(F32).astype(jnp.int32)
    owner = meta_ref[:, LANES // 2 : LANES // 2 + 1] // resident
    x = lax.axis_index("adapter")
    for t in range(out_ref.shape[0]):
        picked = queries[0][t]
        for j in range(1, adapters):
            picked = jnp.where(owner == peer(x, j, adapters), queries[j][t], picked)
        out_ref[t] = picked


def load_queries(query_ref, rows_ref):
    steps, rows, _ = query_ref.shape
    rows_ref[...] = jnp.zeros_like(rows_ref)
    for t in range(steps):
        rows_ref[t * rows : (t + 1) * rows, :] = query_ref[t].astype(F32)


def group_queries(rows_ref, first, group):
    pieces = [
        rows_ref[:, first + g * HEAD_SIZE : first + (g + 1) * HEAD_SIZE] for g in range(group)
    ]
    return jnp.concatenate(pieces, axis=0).astype(BF16)


def attend(queries, keys, values, scale):
    scores = []
    for query, parts in zip(queries, keys):
        found = []
        for key, bias in parts:
            part = dot(query, key, ((1,), (1,)))
            found.append(part if bias is None else part + bias)
        scores.append(found[0] if len(found) == 1 else jnp.concatenate(found, axis=1))
    peaks = [jnp.max(score, axis=1, keepdims=True) * scale for score in scores]
    weights = [jnp.exp2(s * scale - p).astype(BF16) for s, p in zip(scores, peaks)]
    for weight, peak, parts in zip(weights, peaks, values):
        value = parts[0] if len(parts) == 1 else jnp.concatenate(parts, axis=0)
        ones = jnp.ones((value.shape[0], LANES), BF16)
        summed = dot(weight, jnp.concatenate([value, ones], axis=1), ((1,), (0,)))
        total = summed[:, HEAD_SIZE:]
        yield summed[:, :HEAD_SIZE] * (1.0 / total), peak + jnp.log2(total)


def split_stat(stat, heads):
    first = stat.astype(BF16).astype(F32)
    second = (stat - first).astype(BF16).astype(F32)
    third = stat - first - second
    lane = lax.broadcasted_iota(jnp.int32, stat.shape, 1)
    out = jnp.where(lane < heads, first, 0.0)
    out = jnp.where((lane >= heads) & (lane < 2 * heads), pltpu.roll(second, heads, 1), out)
    out = jnp.where(
        (lane >= 2 * heads) & (lane < 3 * heads), pltpu.roll(third, 2 * heads, 1), out
    )
    return out


def far_kernel(scale, query_ref, kv_ref, out_ref, rows_ref, kept, stats_ref):
    steps, rows, width = query_ref.shape
    heads = width // HEAD_SIZE
    kv_heads = kv_ref.shape[2] // HEAD_SIZE
    group = heads // kv_heads
    cut = rows_ref.shape[0]
    load_queries(query_ref, rows_ref)
    columns = [slice(kv * HEAD_SIZE, (kv + 1) * HEAD_SIZE) for kv in range(kv_heads)]
    found = attend(
        [group_queries(rows_ref, kv * group * HEAD_SIZE, group) for kv in range(kv_heads)],
        [[(kv_ref[0, :, at], None)] for at in columns],
        [[kv_ref[1, :, at]] for at in columns],
        scale,
    )
    stats_ref[...] = split_stat(collect(found, kept, cut, group), heads)
    for t in range(steps):
        at = t * rows
        out_ref[t, :, :width] = kept[at : at + rows, :].astype(BF16)
        out_ref[t, :, width:] = stats_ref[at : at + rows, :].astype(BF16)


def collect(found, kept, cut, group):
    lane = lax.broadcasted_iota(jnp.int32, (cut, LANES), 1)
    stats = jnp.zeros((cut, LANES), F32)
    for kv, (result, level) in enumerate(found):
        for g in range(group):
            head = kv * group + g
            kept[:, head * HEAD_SIZE : (head + 1) * HEAD_SIZE] = result[g * cut : (g + 1) * cut]
            stats = jnp.where(lane == head, level[g * cut : (g + 1) * cut], stats)
    return stats


def near_kernel(scale, query_ref, kv_ref, suffix_ref, fresh_ref, meta_ref, *refs):
    own_ref, level_ref, rows_ref, kept, stats, fresh_rows, length_rows = refs
    load_queries(query_ref, rows_ref)
    steps, rows, width = query_ref.shape
    heads = width // HEAD_SIZE
    kv_heads = kv_ref.shape[2] // HEAD_SIZE
    group = heads // kv_heads
    cut = rows_ref.shape[0]
    fresh_rows[...] = jnp.zeros_like(fresh_rows)
    length_rows[...] = jnp.zeros_like(length_rows)
    for t in range(steps):
        length_rows[t * rows : (t + 1) * rows, :] = meta_ref[...]
        for part in range(2):
            fresh_rows[part, t * rows : (t + 1) * rows, :] = fresh_ref[part, t].astype(F32)
    slots = suffix_ref.shape[2]
    suffix_count = rows * slots
    shape = (cut, suffix_count + fresh_rows.shape[1])
    token = lax.broadcasted_iota(jnp.int32, shape, 0)
    column = lax.broadcasted_iota(jnp.int32, shape, 1)
    token_row, token_step = token % rows, token // rows
    fresh_at = column - suffix_count
    in_suffix = (column < suffix_count) & (column // slots == token_row)
    in_suffix &= column % slots < length_rows[:, 0:1]
    in_fresh = (column >= suffix_count) & (fresh_at % rows == token_row)
    in_fresh &= fresh_at // rows <= token_step
    bias = jnp.where(in_suffix | in_fresh, 0.0, MASKED)
    bias = jnp.concatenate([bias] * group, axis=0)
    columns = [slice(kv * HEAD_SIZE, (kv + 1) * HEAD_SIZE) for kv in range(kv_heads)]

    def local(part, at):
        pieces = [suffix_ref[part, r, :, at] for r in range(rows)]
        return jnp.concatenate(pieces + [fresh_rows[part, :, at].astype(BF16)], axis=0)

    found = attend(
        [group_queries(rows_ref, kv * group * HEAD_SIZE, group) for kv in range(kv_heads)],
        [[(kv_ref[0, :, at], None), (local(0, at), bias)] for at in columns],
        [[kv_ref[1, :, at], local(1, at)] for at in columns],
        scale,
    )
    stats[...] = collect(found, kept, cut, group)
    for t in range(steps):
        own_ref[t] = kept[t * rows : (t + 1) * rows, :]
        level_ref[t] = stats[t * rows : (t + 1) * rows, :]


def message_levels(packed, heads):
    count = packed.shape[1]
    return (
        packed + pltpu.roll(packed, count - heads, 1) + pltpu.roll(packed, count - 2 * heads, 1)
    )


def mix(own_ref, level_ref, arrived, store, finish=None):
    steps, _, width = own_ref.shape
    heads = width // HEAD_SIZE
    shares, levels = [], []
    for t in range(steps):
        parts = [level_ref[t]]
        for ref in arrived:
            parts.append(message_levels(ref[t, :, width:].astype(F32), heads))
        highest = functools.reduce(jnp.maximum, parts)
        weights = [jnp.exp2(part - highest) for part in parts]
        total = functools.reduce(jnp.add, weights)
        inverse = 1.0 / total
        shares.append([weight * inverse for weight in weights])
        levels.append(highest + jnp.log2(total))
    quarter = heads // 4 if heads % 4 == 0 else heads
    for h in range(heads):
        at = slice(h * HEAD_SIZE, (h + 1) * HEAD_SIZE)
        for t in range(steps):
            mixed = own_ref[t, :, at] * shares[t][0][:, h : h + 1]
            for ref, share in zip(arrived, shares[t][1:]):
                mixed += ref[t, :, at].astype(F32) * share[:, h : h + 1]
            store(t, at, mixed)
        if finish and (h + 1) % quarter == 0:
            finish(slice((h + 1 - quarter) * HEAD_SIZE, (h + 1) * HEAD_SIZE))
    return levels


def blend_kernel(*refs):
    arrived = refs[:-4]
    own_ref, level_ref, out_ref, out_level_ref = refs[-4:]

    def store(t, at, mixed):
        out_ref[t, :, at] = mixed

    for t, level in enumerate(mix(own_ref, level_ref, arrived, store)):
        out_level_ref[t] = level


def merge_kernel(messages, adapters, *refs):
    arrived = refs[:messages]
    own_ref, level_ref = refs[messages : messages + 2]
    downs = refs[2 + messages : 2 + messages + adapters]
    meta_ref, out_ref, rank_ref, rows_ref, ids_ref = refs[2 + messages + adapters :]
    steps, rows, _ = own_ref.shape
    resident, rank, _ = downs[0].shape
    depth = resident * rank
    x = lax.axis_index("adapter")
    rows_ref[...] = jnp.zeros_like(rows_ref)
    ids_ref[...] = jnp.zeros_like(ids_ref)
    for t in range(steps):
        ids_ref[t * rows : (t + 1) * rows, :] = meta_ref[...]
    products = []

    def store(t, at, mixed):
        out_ref[t, :, at] = mixed.astype(BF16)
        rows_ref[t * rows : (t + 1) * rows, at] = mixed

    def finish(at):
        factors = [down[u, :, at] for down in downs for u in range(resident)]
        products.append(
            dot(rows_ref[:, at].astype(BF16), jnp.concatenate(factors, axis=0), ((1,), (1,)))
        )

    mix(own_ref, level_ref, arrived, store, finish)
    result = functools.reduce(jnp.add, products)
    lane = lax.broadcasted_iota(jnp.int32, result.shape, 1)
    owner = peer(x, lane // depth, adapters) * resident + lane % depth // rank
    rank_ref[...] = jnp.where(owner == ids_ref[:, LANES // 2 : LANES // 2 + 1], result, 0.0)


def up_kernel(parts, adapters, *refs):
    ranks = refs[:parts]
    ups = refs[parts : parts + adapters]
    attended_ref, attended_hbm, out_hbm, out_ref, sems = refs[parts + adapters :]
    copies = [pltpu.make_async_copy(attended_ref, attended_hbm, sems.at[4])]
    copies[0].start()
    steps, rows, width = out_ref.shape
    resident = ups[0].shape[0]
    chosen = functools.reduce(jnp.add, [ref[...] for ref in ranks]).astype(BF16)
    quarter = width // 4
    for i in range(4):
        at = slice(i * quarter, (i + 1) * quarter)
        factors = jnp.concatenate([up[u, :, at] for up in ups for u in range(resident)], axis=0)
        result = dot(chosen, factors, ((1,), (0,)))
        for t in range(steps):
            out_ref[t, :, at] = result[t * rows : (t + 1) * rows].astype(BF16)
        copy = pltpu.make_async_copy(out_ref.at[:, :, at], out_hbm.at[:, :, at], sems.at[i])
        copy.start()
        copies.append(copy)
    for copy in copies:
        copy.wait()


def rope_table(slots, first_position):
    half_dim = HEAD_SIZE // 2
    frequency = rope_base ** (-2.0 * jnp.arange(half_dim, dtype=F32) / HEAD_SIZE)
    position = (first_position + jnp.arange(slots, dtype=jnp.int32)).astype(F32)
    angles = position[:, None] * frequency
    cos_part, sin_part = jnp.cos(angles), jnp.sin(angles)
    return jnp.concatenate([cos_part, cos_part, -sin_part, sin_part], axis=1)


def on_device(
    hidden,
    base_query_rows,
    fresh_key_value,
    suffix_key_value,
    suffix_length,
    row_adapter_index,
    prompt_key_value,
    query_down_factors,
    query_up_factors,
    output_down_factors,
    output_up_factors,
):
    rows, steps, width = hidden.shape
    seq_count, adapters, halves = (lax.axis_size(name) for name in ("seq", "adapter", "head"))
    slots = suffix_key_value.shape[2]
    resident, rank, _ = query_down_factors.shape
    depth = resident * rank
    tokens = rows * steps
    pad_rows = -(-tokens // 16) * 16
    heads = width // HEAD_SIZE
    kv_heads = prompt_key_value.shape[2] // HEAD_SIZE
    group = heads // kv_heads
    scale = math.log2(math.e) / math.sqrt(HEAD_SIZE)
    stat_lanes = -(-3 * heads // LANES) * LANES
    hidden = hidden.transpose(1, 0, 2)
    lane = lax.broadcasted_iota(jnp.int32, (steps, rows, width + LANES), 2)
    facts = jnp.where(lane < width + LANES // 2, suffix_length[:, None], row_adapter_index)
    base = jnp.pad(base_query_rows.transpose(1, 0, 2), ((0, 0), (0, 0), (0, LANES)))
    base = jnp.where(lane < width, base, facts.astype(BF16))
    fresh = fresh_key_value.transpose(0, 2, 1, 3)

    own_rows = jax.ShapeDtypeStruct((pad_rows, depth), F32)
    factors = jax.ShapeDtypeStruct(query_down_factors.shape, BF16)
    first = call(first_kernel, jax.ShapeDtypeStruct((8, LANES), F32), (), flops=1 << 34)
    table_slots = -(-(slots + steps) // 16) * 16
    table = rope_table(table_slots, prompt_key_value.shape[1] * seq_count)
    own_ranks, own_down, table = call(
        own_rank_kernel,
        (own_rows, factors, jax.ShapeDtypeStruct((table_slots, 6 * LANES), BF16)),
        (hidden, query_down_factors, table, first),
        scratch=[pltpu.VMEM((pad_rows, width), F32)],
    )
    hidden_of = [fetch(hidden, "adapter", j) for j in range(1, adapters)]
    ranks = call(
        functools.partial(rank_kernel, adapters - 1),
        jax.ShapeDtypeStruct((adapters * pad_rows, depth), F32),
        (*hidden_of, own_down, own_ranks),
        scratch=[pltpu.VMEM(((adapters - 1) * pad_rows, width), F32)],
    )
    rank_parts = [ranks] + [fetch(ranks, "head", j) for j in range(1, halves)]
    own_up = call(
        copy_kernel,
        jax.ShapeDtypeStruct(query_up_factors.shape, BF16),
        (query_up_factors, ranks),
    )
    block_queries = []
    for j in reversed(range(adapters)):
        block_base = fetch(base, "adapter", j) if j else base
        block_queries.insert(
            0,
            call(
                functools.partial(query_kernel, halves, j),
                jax.ShapeDtypeStruct((steps, rows, width), BF16),
                (
                    *rank_parts,
                    own_up,
                    block_base,
                    table,
                    *block_queries[:1],
                ),
                scratch=[
                    pltpu.VMEM((pad_rows, LANES), F32),
                    pltpu.VMEM((pad_rows, 2 * LANES), F32),
                ],
            ),
        )
    arrived = [send(part, "adapter", j) for j, part in enumerate(block_queries) if j]
    output_down_factors, output_up_factors, token = lax.optimization_barrier(
        (output_down_factors, output_up_factors, block_queries[0][0, :, :LANES])
    )
    queries, meta = call(
        functools.partial(pick_kernel, adapters, resident),
        (
            jax.ShapeDtypeStruct((steps, rows, width), BF16),
            jax.ShapeDtypeStruct((rows, LANES), jnp.int32),
        ),
        (block_queries[0], *arrived, base, token),
        flops=1 << 36,
    )
    message = jax.ShapeDtypeStruct((steps, rows, width + stat_lanes), BF16)
    query_scratch = [
        pltpu.VMEM((pad_rows, width), F32),
        pltpu.VMEM((pad_rows, width), F32),
        pltpu.VMEM((pad_rows, LANES), F32),
    ]
    piece_of = {0: queries}
    for k in range(1, seq_count):
        piece_of[k] = fetch(piece_of[k - 1], "seq", 1) if k % 2 else fetch(queries, "seq", k)
    order = list(range(2, seq_count)) + [1]
    messages = []
    for k in order:
        messages.append(
            call(
                functools.partial(far_kernel, scale),
                message,
                (piece_of[k], prompt_key_value),
                scratch=query_scratch,
            )
        )
    fresh_slots = -(-tokens // LANES) * LANES
    part_shapes = (
        jax.ShapeDtypeStruct((steps, rows, width), F32),
        jax.ShapeDtypeStruct((steps, rows, LANES), F32),
    )
    own, level = call(
        functools.partial(near_kernel, scale),
        part_shapes,
        (queries, prompt_key_value, suffix_key_value, fresh, meta),
        scratch=query_scratch
        + [
            pltpu.VMEM((2, fresh_slots, fresh.shape[3]), F32),
            pltpu.VMEM((pad_rows, LANES), jnp.int32),
        ],
    )
    output_downs = [output_down_factors] + [
        fetch(output_down_factors, "adapter", j) for j in range(1, adapters)
    ]
    output_ups = [output_up_factors] + [
        fetch(output_up_factors, "adapter", j) for j in range(1, adapters)
    ]
    partials = [send(part, "seq", k) for part, k in zip(messages, order)]
    last = max(seq_count - 3, 0)
    early, partials = partials[:last] + partials[last + 1 :], partials[last : last + 1]
    if early:
        own, level = call(blend_kernel, part_shapes, (*early, own, level))
    attended, out_rank = call(
        functools.partial(merge_kernel, len(partials), adapters),
        (
            jax.ShapeDtypeStruct((steps, rows, width), BF16),
            jax.ShapeDtypeStruct((pad_rows, adapters * depth), F32),
        ),
        (*partials, own, level, *output_downs, meta),
        scratch=[
            pltpu.VMEM((pad_rows, width), F32),
            pltpu.VMEM((pad_rows, LANES), jnp.int32),
        ],
    )
    out_ranks = [out_rank] + [fetch(out_rank, "head", j) for j in range(1, halves)]
    attended, adapted = call(
        functools.partial(up_kernel, halves, adapters),
        (jax.ShapeDtypeStruct((steps, rows, width), BF16),) * 2,
        (*out_ranks, *output_ups, attended),
        scratch=[pltpu.VMEM((steps, rows, width), BF16), pltpu.SemaphoreType.DMA((5,))],
        out_specs=(pl.BlockSpec(memory_space=pl.ANY),) * 2,
    )
    return attended.transpose(1, 0, 2), adapted.transpose(1, 0, 2)


def solution(mesh):
    rows = ("groups", "seq", "adapter")
    factors = P(("groups", "adapter"), None, "head")
    placed = (
        P(rows, None, "head"),
        P(rows, None, "head"),
        P(None, rows, None, "head"),
        P(None, rows, None, "head"),
        P(rows),
        P(rows, None),
        P(None, ("groups", "seq"), "head"),
        factors,
        factors,
        factors,
        factors,
    )
    return jax.shard_map(
        on_device,
        mesh=mesh,
        in_specs=placed,
        out_specs=(P(rows, None, "head"), P(rows, None, "head")),
        check_vma=False,
    )
```
